32 devices in a mesh: rep: 2 (over x), tp: 16 (over z, y, core).
Axes of the slice: x: 2, y: 2, z: 4, core: 2. Of those that a mesh axis runs over, the one named last changes fastest.
Arguments:
- queries: bfloat16 [4, 256, 8192], P(None, 'rep', 'tp'), parts along dimension 1, may hold values from -80 to 80
- key_cache: bfloat16 [256, 12, 1024], P('rep'), parts along dimension 0, may hold values from -4 to 4
- value_cache: bfloat16 [256, 12, 1024], P('rep'), parts along dimension 0, may hold values from -5 to 5
- new_keys: bfloat16 [4, 256, 1024], P(None, 'rep'), parts along dimension 1, may hold values from -5 to 5
- new_values: bfloat16 [4, 256, 1024], P(None, 'rep'), parts along dimension 1, may hold values from -5 to 5
- cache_lengths: int32 [256], P('rep'), parts along dimension 0, may hold values from 2 to 12, as said below
- adapter_ids: int32 [256, 1], P('rep'), parts along dimension 0, may hold values from 0 to 15
- out_weight: bfloat16 [8192, 8192], P('tp'), may hold values from -0.0625 to 0.0625
- shrink_panels: bfloat16 [16, 64, 8192], P('tp'), may hold values from -0.0625 to 0.0625
- expand_panels: bfloat16 [16, 64, 8192], P('tp'), may hold values from -0.75 to 0.75
Outputs:
- outputs: bfloat16 [4, 256, 8192], P(None, 'rep', 'tp'), parts along dimension 1
The draws below stay inside these ranges and needn't reach their ends.
There are 2 independent parts, one for each index of `rep`. The reference program is written for one: setup_inputs(seed, part) draws one part's arguments, and reference() takes and returns one part's arrays. A program takes and returns all parts, laid end to end along the dimension named above; an argument that names none is the same for every part. Nothing has to cross between parts.
Inputs may be any that keep to these rules, and one draw needn't show every extreme that they name: `cache_lengths`: some request has all 12 positions. `adapter_ids`: every adapter serves some request.
All inputs are finite; a program needn't handle non-finite values.
Results may differ from the reference program's by a relative error of at most 0.006.
Values may be sent and summed in bfloat16 or wider, within the bound.
No kernel may reach another device: no remote copies, remote signals or barrier semaphores. Data moves between devices by JAX's collectives and lax.ppermute only.
A program may use at most 128 MiB of HBM per device.

```python
import jax
import jax.numpy as jnp
from jax import lax

D = 8192
HEADS = 64
KV_HEADS = 8
HD = 128
RANK = 64
STEPS = 4
REQ = 128
L = 12
GROUP = 8
KV_DIM = 1024
ADAPTERS = 16


def cache_shared(key):
    return jnp.clip(jax.random.normal(key, (REQ, L, KV_DIM), jnp.float32), -4.0, 4.0)


def draw_key_cache(key, part):
    shared = cache_shared(key)
    return shared.astype(jnp.bfloat16)


def draw_queries(key, part):
    key = jax.random.fold_in(key, 5)
    fresh_draw = jnp.clip(jax.random.normal(key, (STEPS, REQ, D), jnp.float32), -4.0, 4.0)
    return fresh_draw.astype(jnp.bfloat16)


def draw_cache_lengths(key, part):
    key = jax.random.fold_in(key, 7)
    drawn = jax.random.randint(key, (REQ,), 2, L + 1, dtype=jnp.int32)
    return drawn.at[0].set(L)


def levels(rng, dims, shards, smallest, top_value):
    factor_of = 1.0
    for position, blocks in shards:
        heights = jax.random.uniform(jax.random.fold_in(jax.random.fold_in(rng, 6), position), (blocks,), jnp.float32, smallest / len(shards), top_value / len(shards))
        factor_of = factor_of * jnp.repeat(jnp.exp(heights), dims[position] // blocks).reshape((-1,) + (1,) * (len(dims) - 1 - position))
    return factor_of


def distinct(key, rows, count, top, lift):
    order = jax.random.permutation(jax.random.fold_in(key, 1), count)
    pull = order
    for power in range(3):
        pull = pull * pull // count
    pull = pull * lift // count
    chance = jax.random.randint(jax.random.fold_in(key, 2), (rows, count), 0, 4096) + pull
    fixed_rows = jax.random.permutation(jax.random.fold_in(key, 3), rows)[jnp.arange(count) % rows]
    chance = jnp.where(jnp.arange(rows)[:, None] == fixed_rows[None, :], 1 << 14, chance)
    score = chance * count + jnp.arange(count)
    return lax.top_k(score.astype(jnp.int32), top)[1].astype(jnp.int32)


def noise(rng, extent, spread, limit, split=(), kind=jnp.bfloat16):
    level = levels(rng, extent, split, -0.22, 0.18) if split else 1.0
    values = jax.random.normal(rng, extent, jnp.float32) * spread * level
    return jnp.minimum(jnp.maximum(values, -limit), limit).astype(kind)


def setup_inputs(seed: int = 0, part: int = 0) -> dict:
    key_of = jax.random.split(jax.random.key(seed), 11)
    part_splits = jax.random.split(jax.random.fold_in(key_of[10], part), 11)
    queries = draw_queries(jax.random.fold_in(jax.random.fold_in(key_of[10], part), 71), part)
    key_cache = draw_key_cache(jax.random.fold_in(jax.random.fold_in(key_of[10], part), 71), part)
    value_cache = noise(part_splits[2], (REQ, L, KV_DIM), 1.0, 5.0)
    new_keys = noise(part_splits[3], (STEPS, REQ, KV_DIM), 1.0, 5.0)
    new_values = noise(part_splits[4], (STEPS, REQ, KV_DIM), 1.0, 5.0)
    cache_lengths = draw_cache_lengths(jax.random.fold_in(jax.random.fold_in(key_of[10], part), 71), part)
    adapter_ids = distinct(part_splits[6], REQ, ADAPTERS, 1, 1024)
    out_weight = noise(key_of[7], (D, D), D ** -0.5, 0.0625, ((0, 16),))
    shrink_panels = noise(key_of[8], (ADAPTERS, RANK, D), D ** -0.5, 0.0625, ((0, 16),))
    expand_panels = noise(key_of[9], (ADAPTERS, RANK, D), RANK ** -0.5, 0.75, ((0, 16),))
    return {"queries": queries, "key_cache": key_cache, "value_cache": value_cache, "new_keys": new_keys, "new_values": new_values, "cache_lengths": cache_lengths, "adapter_ids": adapter_ids, "out_weight": out_weight, "shrink_panels": shrink_panels, "expand_panels": expand_panels}


def attend_all(query, keys, values, fresh_keys, fresh_values, visible, single_decode_pass):
    request_count = query.shape[0]
    query_heads = query.astype(jnp.float32).reshape(request_count, HEADS, HD)
    key_heads = jnp.repeat(keys.astype(jnp.float32).reshape(request_count, L, KV_HEADS, HD), GROUP, axis=2)
    value_heads = jnp.repeat(values.astype(jnp.float32).reshape(request_count, L, KV_HEADS, HD), GROUP, axis=2)
    new_key_heads = jnp.repeat(fresh_keys[:single_decode_pass + 1].astype(jnp.float32).reshape(single_decode_pass + 1, request_count, KV_HEADS, HD), GROUP, axis=2)
    new_value_heads = jnp.repeat(fresh_values[:single_decode_pass + 1].astype(jnp.float32).reshape(single_decode_pass + 1, request_count, KV_HEADS, HD), GROUP, axis=2)
    score_scale = 1.0 / jnp.sqrt(jnp.float32(HD))
    cached_scores = jnp.einsum('rhd,rphd->rhp', query_heads, key_heads) * score_scale
    cached_scores = jnp.where(visible[:, None, :], cached_scores, jnp.float32(-1e+30))
    fresh_scores = jnp.einsum('rhd,srhd->rhs', query_heads, new_key_heads) * score_scale
    highest = jnp.maximum(cached_scores.max(-1), fresh_scores.max(-1))
    cached_exp = jnp.exp(cached_scores - highest[..., None])
    fresh_exp = jnp.exp(fresh_scores - highest[..., None])
    denominator = cached_exp.sum(-1) + fresh_exp.sum(-1)
    cached_weights = (cached_exp / denominator[..., None]).astype(jnp.bfloat16).astype(jnp.float32)
    fresh_weights = (fresh_exp / denominator[..., None]).astype(jnp.bfloat16).astype(jnp.float32)
    attended = jnp.einsum('rhp,rphd->rhd', cached_weights, value_heads) + jnp.einsum('rhs,srhd->rhd', fresh_weights, new_value_heads)
    return attended.reshape(request_count, HEADS * HD).astype(jnp.bfloat16)

def reference(queries, key_cache, value_cache, new_keys, new_values, cache_lengths, adapter_ids, out_weight, shrink_panels, expand_panels):
    positions = jnp.arange(L, dtype=jnp.int32)
    visible = positions[None, :] < cache_lengths[:, None]
    chosen = (adapter_ids == jnp.arange(ADAPTERS, dtype=jnp.int32)[None, :]).astype(jnp.float32)
    shrink_flat = shrink_panels.reshape(ADAPTERS * RANK, D)
    expand_flattened = expand_panels.reshape(ADAPTERS * RANK, D)
    step_outputs = []
    for single_decode_pass in range(STEPS):
        attended = attend_all(queries[single_decode_pass], key_cache, value_cache, new_keys, new_values, visible, single_decode_pass)
        base_product = jnp.dot(attended, out_weight, preferred_element_type=jnp.float32)
        all_ranks = jnp.dot(attended, shrink_flat.T, preferred_element_type=jnp.float32)
        shrunk = (all_ranks.reshape(REQ, ADAPTERS, RANK) * chosen[:, :, None]).sum(1).astype(jnp.bfloat16)
        distribute_rows = (chosen[:, :, None] * shrunk[:, None, :].astype(jnp.float32)).reshape(REQ, ADAPTERS * RANK).astype(jnp.bfloat16)
        adapter_product = jnp.dot(distribute_rows, expand_flattened, preferred_element_type=jnp.float32)
        step_outputs.append((base_product + adapter_product).astype(jnp.bfloat16))
    return jnp.stack(step_outputs)
```

```python
import functools

import jax
import jax.numpy as jnp
from jax import lax
from jax.experimental import pallas as pl
from jax.experimental.pallas import tpu as pltpu
from jax.sharding import PartitionSpec as P

HD = 128
GROUP_REQ = 16
ROW_CHUNKS = (128, 128, 128, 128)
F32 = jnp.float32
BF16 = jnp.bfloat16


def attention_kernel(head_ref, q_ref, kc_ref, vc_ref, nk_ref, nv_ref, limit_ref, out_ref):
    steps, block_req, width = q_ref.shape
    heads = width // HD
    cached, fresh = kc_ref.shape[0], nk_ref.shape[0]
    group = GROUP_REQ
    rows, columns = steps * heads * group, (cached + fresh) * group
    row = lax.broadcasted_iota(jnp.int32, (rows, columns), 0)
    column = lax.broadcasted_iota(jnp.int32, (rows, columns), 1)
    same = row % group == column % group
    position = column // group
    step = row // (heads * group)
    fresh_ok = jnp.logical_and(position >= cached, position - cached <= step)
    column_position = lax.broadcasted_iota(jnp.int32, (1, columns), 1) // group
    for i in range(block_req // group):
        span = slice(i * group, (i + 1) * group)
        query = jnp.concatenate(
            [q_ref[s, span, h * HD : (h + 1) * HD] for s in range(steps) for h in range(heads)], 0
        )
        keys = jnp.concatenate(
            [kc_ref[p, span, :] for p in range(cached)] + [nk_ref[s, span, :] for s in range(fresh)], 0
        )
        values = jnp.concatenate(
            [vc_ref[p, span, :] for p in range(cached)] + [nv_ref[s, span, :] for s in range(fresh)], 0
        )
        scores = lax.dot_general(
            query, keys, (((1,), (1,)), ((), ())), preferred_element_type=F32
        ) * (1.0 / HD**0.5)
        cached_ok = column_position < limit_ref[i, :, :]
        visible = jnp.logical_and(same, jnp.logical_or(cached_ok, fresh_ok))
        scores = jnp.where(visible, scores, -1e30)
        scaled = jnp.exp(scores - scores.max(-1, keepdims=True))
        weights = (scaled / scaled.sum(-1, keepdims=True)).astype(BF16)
        mixed = jnp.dot(weights, values, preferred_element_type=F32).astype(BF16)
        for s in range(steps):
            for h in range(heads):
                at = (s * heads + h) * group
                out_ref[s, span, h * HD : (h + 1) * HD] = mixed[at : at + group, :]


def attend(queries, key_cache, value_cache, new_keys, new_values, cache_lengths, head):
    steps, requests, width = queries.shape
    cached = key_cache.shape[1]
    columns = (cached + steps) * GROUP_REQ
    limits = jnp.tile(cache_lengths.reshape(-1, 1, GROUP_REQ), (1, 1, cached + steps))
    block = requests // 2
    grid_spec = pltpu.PrefetchScalarGridSpec(
        num_scalar_prefetch=1,
        grid=(requests // block,),
        in_specs=[
            pl.BlockSpec((steps, block, width), lambda i, head: (0, i, 0)),
            pl.BlockSpec((cached, block, HD), lambda i, head: (0, i, head[0])),
            pl.BlockSpec((cached, block, HD), lambda i, head: (0, i, head[0])),
            pl.BlockSpec((steps, block, HD), lambda i, head: (0, i, head[0])),
            pl.BlockSpec((steps, block, HD), lambda i, head: (0, i, head[0])),
            pl.BlockSpec((block // GROUP_REQ, 1, columns), lambda i, head: (i, 0, 0)),
        ],
        out_specs=pl.BlockSpec((steps, block, width), lambda i, head: (0, i, 0)),
    )
    return pl.pallas_call(
        attention_kernel,
        grid_spec=grid_spec,
        out_shape=jax.ShapeDtypeStruct(queries.shape, BF16),
        compiler_params=pltpu.CompilerParams(vmem_limit_bytes=32 << 20),
        cost_estimate=pl.CostEstimate(
            flops=4 * requests * steps * width * columns, bytes_accessed=4 << 20, transcendentals=0
        ),
        name="attention",
    )(
        head.reshape(1),
        queries,
        key_cache.transpose(1, 0, 2),
        value_cache.transpose(1, 0, 2),
        new_keys,
        new_values,
        limits,
    )


def project_kernel(index_ref, a_ref, w_ref, send_ref, keep_ref):
    width = keep_ref.shape[2]
    mine = index_ref[0] % 2
    keep = pl.multiple_of(mine * width, width)
    send = pl.multiple_of((1 - mine) * width, width)
    a = a_ref[...]
    send_ref[0] = jnp.dot(a, w_ref[:, pl.ds(send, width)], preferred_element_type=F32).astype(BF16)
    keep_ref[0] = jnp.dot(a, w_ref[:, pl.ds(keep, width)], preferred_element_type=F32)


def project(index, attended, weight, first_row, rows, pairs, odd):
    depth, full = weight.shape
    width = full // (2 * pairs)
    unit = first_row // rows
    grid_spec = pltpu.PrefetchScalarGridSpec(
        num_scalar_prefetch=1,
        grid=(pairs // 2,),
        in_specs=[
            pl.BlockSpec((rows, depth), lambda i, index: (unit, 0)),
            pl.BlockSpec((depth, 2 * width), lambda i, index: (0, (2 * i + odd) ^ (index[0] // 2))),
        ],
        out_specs=[
            pl.BlockSpec((1, rows, width), lambda i, index: (i, 0, 0)),
            pl.BlockSpec((1, rows, width), lambda i, index: (i, 0, 0)),
        ],
    )
    return pl.pallas_call(
        project_kernel,
        grid_spec=grid_spec,
        out_shape=[
            jax.ShapeDtypeStruct((pairs // 2, rows, width), BF16),
            jax.ShapeDtypeStruct((pairs // 2, rows, width), F32),
        ],
        compiler_params=pltpu.CompilerParams(vmem_limit_bytes=32 << 20),
        cost_estimate=pl.CostEstimate(
            flops=rows * depth * full,
            bytes_accessed=depth * full + 3 * rows * full // 2,
            transcendentals=0,
        ),
        name="project",
    )(index.reshape(1), attended, weight)


def shrink_kernel(ids_ref, a_ref, panel_ref, out_ref):
    rank = out_ref.shape[1]
    ranks = lax.dot_general(
        a_ref[...], panel_ref[...], (((1,), (1,)), ((), ())), preferred_element_type=F32
    )
    owner = lax.broadcasted_iota(jnp.int32, ranks.shape, 1) // rank
    ranks = jnp.where(owner == ids_ref[...], ranks, 0.0)
    total = ranks[:, : 2 * rank]
    for i in range(1, ranks.shape[1] // (2 * rank)):
        total = total + ranks[:, 2 * rank * i : 2 * rank * (i + 1)]
    out_ref[...] = total[:, :rank] + total[:, rank:]


def shrink(ids, attended, panels, rank):
    rows = attended.shape[0]
    return pl.pallas_call(
        shrink_kernel,
        out_shape=jax.ShapeDtypeStruct((rows, rank), F32),
        compiler_params=pltpu.CompilerParams(vmem_limit_bytes=48 << 20),
        cost_estimate=pl.CostEstimate(
            flops=2 * rows * panels.shape[0] * panels.shape[1], bytes_accessed=4 << 20, transcendentals=0
        ),
        name="shrink",
    )(ids, attended, panels)


def expand_kernel(ids_ref, shrunk_ref, panel_ref, out_ref):
    rank = shrunk_ref.shape[1]
    shrunk = shrunk_ref[...].astype(BF16).astype(F32)
    spread = jnp.concatenate([shrunk] * (panel_ref.shape[0] // rank), 1)
    owner = lax.broadcasted_iota(jnp.int32, spread.shape, 1) // rank
    spread = jnp.where(owner == ids_ref[...], spread, 0.0).astype(BF16)
    out_ref[...] = jnp.dot(spread, panel_ref[...], preferred_element_type=F32)


def expand(ids, shrunk, panels):
    rows = shrunk.shape[0]
    return pl.pallas_call(
        expand_kernel,
        out_shape=jax.ShapeDtypeStruct((rows, panels.shape[1]), F32),
        compiler_params=pltpu.CompilerParams(vmem_limit_bytes=48 << 20),
        cost_estimate=pl.CostEstimate(
            flops=2 * rows * panels.shape[0] * panels.shape[1], bytes_accessed=4 << 20, transcendentals=0
        ),
        name="expand",
    )(ids, shrunk, panels)


def swap(array, bit, size):
    return lax.ppermute(array, "tp", [(i, i ^ bit) for i in range(size)])


def own_columns(panel, size):
    width = panel.shape[2] // size
    blocks = jnp.concatenate([panel[:, :, i * width : (i + 1) * width] for i in range(size)], 0)
    mine = lax.all_to_all(blocks, "tp", split_axis=0, concat_axis=0, tiled=True)
    return mine.reshape(-1, width)


def body(
    size,
    queries,
    key_cache,
    value_cache,
    new_keys,
    new_values,
    cache_lengths,
    adapter_ids,
    out_weight,
    shrink_panels,
    expand_panels,
):
    steps, requests, local = queries.shape
    rank = shrink_panels.shape[1]
    rows = steps * requests
    index = lax.axis_index("tp")
    group = size * local // key_cache.shape[2]
    head = index * (local // HD) // group
    shrink_own = own_columns(shrink_panels, size)
    expand_own = own_columns(expand_panels, size)
    ids = jnp.tile(adapter_ids, (steps, 1))
    attended = attend(
        queries, key_cache, value_cache, new_keys, new_values, cache_lengths, head
    ).reshape(rows, local)

    bits = [1 << b for b in range(size.bit_length() - 1)]
    pairs = size // 2
    sums = []
    first = 0
    for count in ROW_CHUNKS:
        send, keep_far = project(index, attended, out_weight, first, count, pairs, 1)
        far = (keep_far + swap(send, bits[0], size).astype(F32)).astype(BF16)
        far = swap(far, bits[1], size)
        send, keep = project(index, attended, out_weight, first, count, pairs, 0)
        near = swap(send, bits[0], size)
        keep = keep + near.astype(F32) + far.astype(F32)
        for bit in bits[2:]:
            blocks = keep.reshape((keep.shape[0] // 2, 2) + keep.shape[1:])
            arrived = swap(blocks[:, 1].astype(BF16), bit, size)
            keep = blocks[:, 0] + arrived.astype(F32)
        sums.append(keep[0])
        first += count

    shrunk = shrink(ids, attended, shrink_own, rank)
    for bit in bits:
        shrunk = shrunk + swap(shrunk, bit, size)
    lora = expand(ids, shrunk, expand_own)
    total = jnp.concatenate(sums, 0) + lora
    return total.astype(BF16).reshape(queries.shape)


def solution(mesh):
    return jax.shard_map(
        functools.partial(body, mesh.shape["tp"]),
        mesh=mesh,
        in_specs=(
            P(None, "rep", "tp"),
            P("rep", None, None),
            P("rep", None, None),
            P(None, "rep", None),
            P(None, "rep", None),
            P("rep"),
            P("rep", None),
            P("tp", None),
            P("tp", None, None),
            P("tp", None, None),
        ),
        out_specs=P(None, "rep", "tp"),
        check_vma=False,
    )
```

```python
import functools

import jax
import jax.numpy as jnp
from jax import lax
from jax.experimental import pallas as pl
from jax.experimental.pallas import tpu as pltpu
from jax.sharding import PartitionSpec as P

HD = 128
LANES = 128
GROUP_REQ = 16
VMEM_LIMIT = 24 << 20
F32 = jnp.float32
BF16 = jnp.bfloat16
SMALL_PLAN = ((4, (0, 1, 2)), (4, (0, 1, 2)), (2, (0, 1, 2)), (6, (1, 2, 0)))


def call(kernel, name, vmem, hbm, out, cost, after=(), scratch=()):
    operands = [pltpu.with_memory_space_constraint(x, pltpu.VMEM) for x in vmem]
    operands += [pltpu.with_memory_space_constraint(x, pltpu.HBM) for x in hbm]
    count, extra = len(operands), len(after)

    def run(*refs):
        kernel(*refs[:count], *refs[count + extra :])

    return pl.pallas_call(
        run,
        in_specs=[pl.BlockSpec(memory_space=pltpu.VMEM)] * len(vmem)
        + [pl.BlockSpec(memory_space=pltpu.HBM)] * len(hbm)
        + [pl.BlockSpec(memory_space=pl.ANY)] * extra,
        out_specs=[pl.BlockSpec(memory_space=pltpu.VMEM)] * len(out),
        out_shape=[pltpu.VMEM(shape, dtype) for shape, dtype in out],
        scratch_shapes=scratch,
        compiler_params=pltpu.CompilerParams(vmem_limit_bytes=VMEM_LIMIT),
        cost_estimate=pl.CostEstimate(flops=cost, bytes_accessed=1 << 16, transcendentals=0),
        name=name,
    )(*operands, *after)


def put_bit(i, position, value):
    low = i & ((1 << position) - 1)
    return ((i >> position) << (position + 1)) | (value << position) | low


def cut_copies(panel_ref, cut_refs, place, replica):
    groups, share, width = cut_refs[0].shape
    rank = pl.multiple_of(replica * share, share)
    copies = []
    for low, cut_ref in enumerate(cut_refs):
        for high in range(groups):
            column = pl.multiple_of((place ^ (4 * high + low)) * width, width)
            copies.append((panel_ref.at[0, pl.ds(rank, share), pl.ds(column, width)], cut_ref.at[high]))
    return copies


def pick_kernel(w_ref, panel_ref, pick_ref, *rest):
    cut_refs, sems = rest[:-1], rest[-1]
    place, replica = lax.axis_index("tp"), lax.axis_index("rep")
    half, _, width = pick_ref.shape
    pair, other = place // 2, 1 - place % 2
    copies = cut_copies(panel_ref, cut_refs, place, replica)
    for i in range(half):
        column = pl.multiple_of((2 * ((2 * i + 1) ^ pair) + other) * width, width)
        copies.append((w_ref.at[:, pl.ds(column, width)], pick_ref.at[i]))
    copies = [pltpu.make_async_copy(a, b, sems.at[i]) for i, (a, b) in enumerate(copies)]
    for copy in copies:
        copy.start()
    for copy in copies:
        copy.wait()


def pick(weight, panels, pairs, size, replicas):
    depth, full = weight.shape
    width = full // size
    half, share = pairs // 2, panels.shape[1] // replicas
    return call(
        pick_kernel,
        "pick",
        (),
        (weight, panels),
        [((half, depth, width), BF16)] + [((size // 4, share, width), BF16)] * 4,
        0,
        scratch=[pltpu.SemaphoreType.DMA((half + size,))],
    )


def attention_kernel(
    lengths_ref, ids_ref, q_hbm, kc_hbm, vc_hbm, nk_hbm, nv_hbm, w_hbm, panel_hbm,
    out_ref, pick_ref, own_ref, cut0_ref, cut1_ref, cut2_ref, cut3_ref,
    q_ref, kc_ref, vc_ref, nk_ref, nv_ref, q_sems, w_sems,
):
    place, replica = lax.axis_index("tp"), lax.axis_index("rep")
    steps, requests, width = q_ref.shape
    heads = width // HD
    cached, fresh = kc_ref.shape[0], nk_ref.shape[0]
    block = own_ref.shape[2]
    size = 2 * own_ref.shape[0]
    group_heads = size * width // kc_hbm.shape[2]
    head = pl.multiple_of(place * heads // group_heads * HD, HD)
    parts = 2
    part = requests // parts
    loads = []
    for n in range(parts):
        span = pl.ds(n * part, part)
        pieces = [(q_hbm.at[:, span, :], q_ref.at[:, span, :])]
        for a, b in ((kc_hbm, kc_ref), (nk_hbm, nk_ref), (vc_hbm, vc_ref), (nv_hbm, nv_ref)):
            pieces.append((a.at[:, span, pl.ds(head, HD)], b.at[:, span, :]))
        loads.append([pltpu.make_async_copy(a, b, q_sems.at[n, i]) for i, (a, b) in enumerate(pieces)])
    pair, mine = place // 2, place % 2
    others = cut_copies(panel_hbm, (cut0_ref, cut1_ref, cut2_ref, cut3_ref), place, replica)
    for i in range(pick_ref.shape[0]):
        column = pl.multiple_of((2 * ((2 * i) ^ pair) + 1 - mine) * block, block)
        others.append((w_hbm.at[:, pl.ds(column, block)], pick_ref.at[i]))
    for i in range(own_ref.shape[0]):
        column = pl.multiple_of((2 * (i ^ pair) + mine) * block, block)
        others.append((w_hbm.at[:, pl.ds(column, block)], own_ref.at[i]))
    others = [pltpu.make_async_copy(a, b, w_sems.at[i]) for i, (a, b) in enumerate(others)]
    for copy in [c for load in loads for c in load] + others:
        copy.start()

    group = GROUP_REQ
    rows, columns = steps * heads * group, (cached + fresh) * group
    row = lax.broadcasted_iota(jnp.int32, (rows, columns), 0)
    column = lax.broadcasted_iota(jnp.int32, (rows, columns), 1)
    same = row % group == column % group
    position = column // group
    step = row // (heads * group)
    fresh_ok = jnp.logical_and(position >= cached, position - cached <= step)
    column_position = lax.broadcasted_iota(jnp.int32, (1, columns), 1) // group
    tail = lax.broadcasted_iota(jnp.int32, (group, requests), 0) == 0
    out_ref[steps * requests :, :] = jnp.zeros((group, width), BF16)
    out_ref[steps * requests :, :requests] = jnp.where(tail, ids_ref[...].astype(F32), 0.0).astype(BF16)
    for n in range(parts):
        for copy in loads[n]:
            copy.wait()
        for i in range(n * part // group, (n + 1) * part // group):
            span = slice(i * group, (i + 1) * group)
            query = jnp.concatenate(
                [q_ref[s, span, h * HD : (h + 1) * HD] for s in range(steps) for h in range(heads)], 0
            )
            keys = jnp.concatenate(
                [kc_ref[p, span, :] for p in range(cached)] + [nk_ref[s, span, :] for s in range(fresh)], 0
            )
            values = jnp.concatenate(
                [vc_ref[p, span, :] for p in range(cached)] + [nv_ref[s, span, :] for s in range(fresh)], 0
            )
            scores = lax.dot_general(
                query, keys, (((1,), (1,)), ((), ())), preferred_element_type=F32
            ) * (1.0 / HD**0.5)
            limit = jnp.concatenate([lengths_ref[:, span]] * (cached + fresh), 1)
            cached_ok = column_position < limit
            visible = jnp.logical_and(same, jnp.logical_or(cached_ok, fresh_ok))
            scores = jnp.where(visible, scores, -1e30)
            scaled = jnp.exp(scores - scores.max(-1, keepdims=True))
            weights = (scaled / scaled.sum(-1, keepdims=True)).astype(BF16)
            mixed = jnp.dot(weights, values, preferred_element_type=F32).astype(BF16)
            for s in range(steps):
                for h in range(heads):
                    at = (s * heads + h) * group
                    to = s * requests + i * group
                    out_ref[to : to + group, h * HD : (h + 1) * HD] = mixed[at : at + group, :]
    for copy in others:
        copy.wait()


def attend(
    queries, key_cache, value_cache, new_keys, new_values, cache_lengths, adapter_ids, weight, panels, size, replicas, after
):
    steps, requests, width = queries.shape
    cached = key_cache.shape[1]
    depth, full = weight.shape
    block, pairs, share = full // size, size // 2, panels.shape[1] // replicas
    return call(
        attention_kernel,
        "attention",
        (cache_lengths.reshape(1, -1), adapter_ids.reshape(1, -1)),
        (queries, key_cache.transpose(1, 0, 2), value_cache.transpose(1, 0, 2), new_keys, new_values, weight, panels),
        [
            ((steps * requests + GROUP_REQ, width), BF16),
            ((pairs // 2, depth, block), BF16),
            ((pairs, depth, block), BF16),
        ]
        + [((size // 4, share, block), BF16)] * 4,
        4 * requests * steps * width * (cached + steps) * GROUP_REQ,
        after,
        [
            pltpu.VMEM((steps, requests, width), BF16),
            pltpu.VMEM((cached, requests, HD), BF16),
            pltpu.VMEM((cached, requests, HD), BF16),
            pltpu.VMEM((steps, requests, HD), BF16),
            pltpu.VMEM((steps, requests, HD), BF16),
            pltpu.SemaphoreType.DMA((2, 5)),
            pltpu.SemaphoreType.DMA((pairs // 2 + pairs + size,)),
        ],
    )


def product(span, which, a_ref, b_ref, own_ref, odd_ref, even_ref):
    other = (odd_ref if which % 2 else even_ref)[which // 2]
    return jnp.dot(a_ref[span, :], own_ref[which], preferred_element_type=F32) + jnp.dot(
        b_ref[span, :], other, preferred_element_type=F32
    )


def far_kernel(span, stage, *refs):
    operands, out_ref = refs[:-1], refs[-1]
    for i in range(out_ref.shape[0]):
        out_ref[i] = product(span, put_bit(i, stage, 1), *operands).astype(BF16)


def near_kernel(span, stage, following, *refs):
    operands, (arrived_ref, keep_ref, send_ref) = refs[:-3], refs[-3:]
    for i in range(keep_ref.shape[0]):
        for value, out_ref in ((1, send_ref), (0, keep_ref)):
            at = put_bit(i, following, value)
            total = product(span, put_bit(at, stage, 0), *operands) + arrived_ref[at].astype(F32)
            out_ref[i] = total.astype(out_ref.dtype)


def far(span, stage, operands, after):
    pairs, depth, width = operands[2].shape
    rows = span.stop - span.start
    return call(
        functools.partial(far_kernel, span, stage),
        "far",
        operands,
        (),
        [((pairs // 2, rows, width), BF16)],
        2 * rows * depth * pairs * width,
        after,
    )[0]


def near(span, stage, following, operands, arrived, after):
    pairs, depth, width = operands[2].shape
    rows = span.stop - span.start
    return call(
        functools.partial(near_kernel, span, stage, following),
        "near",
        (*operands, arrived),
        (),
        [((pairs // 4, rows, width), F32), ((pairs // 4, rows, width), BF16)],
        2 * rows * depth * pairs * width,
        after,
    )


def add_kernel(following, keep_ref, arrived_ref, more_ref, send_ref):
    for i in range(more_ref.shape[0]):
        for value, out_ref in ((1, send_ref), (0, more_ref)):
            at = put_bit(i, following, value)
            out_ref[i] = (keep_ref[at] + arrived_ref[at].astype(F32)).astype(out_ref.dtype)


def add(following, keep, arrived):
    shape = (keep.shape[0] // 2,) + keep.shape[1:]
    return call(
        functools.partial(add_kernel, following), "add", (keep, arrived), (), [(shape, F32), (shape, BF16)], 2 * keep.size
    )


def sort_kernel(*refs):
    for high, out_ref in enumerate(refs[4:]):
        for low in range(4):
            out_ref[low] = refs[low][high]


def sort(blocks, after):
    groups, share, width = blocks[0].shape
    return call(sort_kernel, "sort", blocks, (), [((4, share, width), BF16)] * groups, 0, after)


def near_blocks(cuts):
    size = 4 * cuts[0].shape[0]
    first = swap(cuts[1], "tp", 1, size)
    second = swap(cuts[3], "tp", 1, size)
    return (cuts[0], first, swap(cuts[2], "tp", 2, size), swap(second, "tp", 2, size)), second


def far_blocks(sorted_blocks):
    size = 4 * len(sorted_blocks)
    return [sorted_blocks[0]] + [swap(b, "tp", 4 * h, size) for h, b in enumerate(sorted_blocks) if h]


def owners(ids, shape, high, share):
    owner = 4 * high + lax.broadcasted_iota(jnp.int32, shape, 1) // share
    return owner == (ids ^ lax.axis_index("tp"))


def shrink_kernel(steps, groups, *refs):
    panels, attended, out_ref = refs[:groups], refs[groups:-1], refs[-1]
    _, share, width = panels[0].shape
    for k, a_ref in enumerate(attended):
        rows = a_ref.shape[0] - GROUP_REQ
        requests = rows // steps
        row = lax.broadcasted_iota(jnp.int32, (requests, requests), 0)
        column = lax.broadcasted_iota(jnp.int32, (requests, requests), 1)
        line = a_ref[rows : rows + GROUP_REQ, :requests].astype(F32)[:1, :]
        ids = jnp.where(row == column, line, 0.0).sum(1, keepdims=True).astype(jnp.int32)
        ids = jnp.concatenate([ids] * steps, 0)
        total = None
        for high, panel in enumerate(panels):
            flat = panel[...].reshape(4 * share, width)
            ranks = lax.dot_general(
                a_ref[:rows, :], flat, (((1,), (1,)), ((), ())), preferred_element_type=F32
            )
            ranks = jnp.where(owners(ids, ranks.shape, high, share), ranks, 0.0)
            total = ranks if total is None else total + ranks
        part = total[:, :share]
        for i in range(1, 4):
            part = part + total[:, share * i : share * (i + 1)]
        fold = out_ref.shape[1]
        out_ref[k] = jnp.concatenate([part[i * fold : (i + 1) * fold] for i in range(rows // fold)], 1)


def shrink(steps, panels, attended, after):
    rows, share = attended[0].shape[0] - GROUP_REQ, panels[0].shape[1]
    return call(
        functools.partial(shrink_kernel, steps, len(panels)),
        "shrink",
        (*panels, *attended),
        (),
        [((len(attended), rows * share // LANES, LANES), F32)],
        2 * rows * len(attended) * len(panels) * panels[0].size,
        after,
    )[0]


def expand_kernel(steps, replicas, ids_ref, *refs):
    ranks, panels, out_ref = refs[:replicas], refs[replicas:-1], refs[-1]
    groups = len(panels) // replicas
    _, share, width = panels[0].shape
    ids = jnp.concatenate([ids_ref[...]] * steps, 0)
    total = None
    for k, rank_ref in enumerate(ranks):
        folded = rank_ref[0].astype(BF16).astype(F32)
        part = jnp.concatenate([folded[:, i * share : (i + 1) * share] for i in range(LANES // share)], 0)
        part = jnp.concatenate([part] * 4, 1)
        for high, panel in enumerate(panels[k * groups : (k + 1) * groups]):
            spread = jnp.where(owners(ids, part.shape, high, share), part, 0.0).astype(BF16)
            term = jnp.dot(spread, panel[...].reshape(4 * share, width), preferred_element_type=F32)
            total = term if total is None else total + term
    out_ref[...] = total


def expand(steps, ids, ranks, panels, after):
    rows, width = steps * ids.shape[0], panels[0].shape[2]
    return call(
        functools.partial(expand_kernel, steps, len(ranks)),
        "expand",
        (ids, *ranks, *panels),
        (),
        [((rows, width), F32)],
        2 * rows * len(panels) * panels[0].size,
        after,
    )[0]


def finish_kernel(spans, lora_ref, *refs):
    out_ref = refs[-1]
    for n, span in enumerate(spans):
        keep_ref, arrived_ref = refs[2 * n : 2 * n + 2]
        out_ref[span, :] = (keep_ref[0] + arrived_ref[0].astype(F32) + lora_ref[span, :]).astype(BF16)


def finish(spans, lora, sums):
    operands = [pltpu.with_memory_space_constraint(x, pltpu.VMEM) for x in (lora, *sums)]
    return pl.pallas_call(
        functools.partial(finish_kernel, spans),
        in_specs=[pl.BlockSpec(memory_space=pltpu.VMEM)] * len(operands),
        out_specs=pl.BlockSpec(memory_space=pltpu.VMEM),
        out_shape=jax.ShapeDtypeStruct(lora.shape, BF16),
        compiler_params=pltpu.CompilerParams(vmem_limit_bytes=VMEM_LIMIT),
        cost_estimate=pl.CostEstimate(flops=4 * lora.size, bytes_accessed=1 << 20, transcendentals=0),
        name="finish",
    )(*operands)


def swap(array, axis, bit, size):
    return lax.ppermute(array, axis, [(i, i ^ bit) for i in range(size)])


def body(
    size,
    replicas,
    queries,
    key_cache,
    value_cache,
    new_keys,
    new_values,
    cache_lengths,
    adapter_ids,
    out_weight,
    shrink_panels,
    expand_panels,
):
    steps, requests, local = queries.shape
    rows = steps * requests
    pairs = size // 2
    stages = size.bit_length() - 2
    plan = SMALL_PLAN if stages == 3 else ((16, tuple(range(stages))),)
    spans, first = [], 0
    for part, _ in plan:
        spans.append(slice(first, first + rows * part // 16))
        first += rows * part // 16

    picked, *cuts = pick(out_weight, shrink_panels, pairs, size, replicas)
    weight_odd = swap(picked, "tp", 1, size)
    shrink_near, ready = near_blocks(cuts)
    attended, picked, weight_own, *cuts = attend(
        queries, key_cache, value_cache, new_keys, new_values, cache_lengths, adapter_ids,
        out_weight, expand_panels, size, replicas, (ready,),
    )
    attended_other = swap(attended, "tp", 1, size)
    weight_even = swap(picked, "tp", 1, size)
    expand_near, ready = near_blocks(cuts)
    attended_all = [attended] + [swap(attended, "rep", k, replicas) for k in range(1, replicas)]
    operands = (attended, attended_other, weight_own, weight_odd, weight_even)

    def begin(n, after):
        order = plan[n][1]
        sent = far(spans[n], order[0], operands, after)
        return sent, swap(sent, "tp", 2 << order[0], size)

    def middle(n, arrived, after):
        order = plan[n][1]
        following = order[1] - (order[1] > order[0])
        keep, send = near(spans[n], order[0], following, operands, arrived, after)
        return keep, send, swap(send, "tp", 2 << order[1], size)

    def end(n, keep, came, after=()):
        order = plan[n][1]
        for i in range(2, stages):
            left = [s - sum(s > t for t in order[: i]) for s in order[i:]]
            keep, send = add(left[0], keep, came)
            came = swap(send, "tp", 2 << order[i], size)
        return [keep, came]

    last = len(plan) - 1
    started, done = {}, {}
    sent, started[0] = begin(0, (ready,))
    shrink_sorted = sort(shrink_near, (sent,))
    shrink_panels = far_blocks(shrink_sorted)
    token = shrink_sorted[0]
    if last:
        token, started[last] = begin(last, (token,))
        token, started[1] = begin(1, (token,))
    expand_sorted = sort(expand_near, (token,))
    expand_panels = far_blocks(expand_sorted)
    expand_all = list(expand_panels)
    for k in range(1, replicas):
        expand_all += [swap(b, "rep", k, replicas) for b in expand_panels]
    keep, token, came = middle(0, started[0], (expand_sorted[0],))
    done[0] = end(0, keep, came)
    shrunk = shrink(steps, shrink_panels, attended_all, (token,))
    token = shrunk
    for bit in (1, 0, *range(2, stages + 1)):
        shrunk = shrunk + swap(shrunk, "tp", 1 << bit, size)
    if last:
        for n in range(2, last):
            token, started[n] = begin(n, (token,))
        for n in (last, *range(1, last)):
            keep, token, came = middle(n, started[n], (token,))
            done[n] = end(n, keep, came)
    ranks = [shrunk[:1]] + [swap(shrunk[k : k + 1], "rep", k, replicas) for k in range(1, replicas)]
    lora = expand(steps, adapter_ids, ranks, expand_all, (token,))
    sums = [x for n in range(last + 1) for x in done[n]]
    return finish(spans, lora, sums).reshape(queries.shape)


def solution(mesh):
    return jax.shard_map(
        functools.partial(body, mesh.shape["tp"], mesh.shape["rep"]),
        mesh=mesh,
        in_specs=(
            P(None, "rep", "tp"),
            P("rep", None, None),
            P("rep", None, None),
            P(None, "rep", None),
            P(None, "rep", None),
            P("rep"),
            P("rep", None),
            P("tp", None),
            P("tp", None, None),
            P("tp", None, None),
        ),
        out_specs=P(None, "rep", "tp"),
        check_vma=False,
    )
```

```python
import functools

import jax
import jax.numpy as jnp
from jax import lax
from jax.experimental import pallas as pl
from jax.experimental.pallas import tpu as pltpu
from jax.sharding import PartitionSpec as P

HD = 128
LANES = 128
GROUP_REQ = 16
VMEM_LIMIT = 24 << 20
F32 = jnp.float32
BF16 = jnp.bfloat16
SMALL_PLAN = ((7, (0, 1, 2)), (6, (0, 1, 2)), (3, (1, 0, 2)))


def call(line, kernel, name, vmem, hbm, out, cost, scratch=(), after=()):
    operands = [pltpu.with_memory_space_constraint(x, pltpu.VMEM) for x in vmem]
    operands += [pltpu.with_memory_space_constraint(x, pltpu.HBM) for x in hbm]
    before = [*line, *after]
    count, extra = len(operands), len(before)

    def run(*refs):
        kernel(*refs[:count], *refs[count + extra :])

    results = pl.pallas_call(
        run,
        in_specs=[pl.BlockSpec(memory_space=pltpu.VMEM)] * len(vmem)
        + [pl.BlockSpec(memory_space=pltpu.HBM)] * len(hbm)
        + [pl.BlockSpec(memory_space=pl.ANY)] * extra,
        out_specs=[pl.BlockSpec(memory_space=pltpu.VMEM)] * len(out),
        out_shape=[pltpu.VMEM(shape, dtype) for shape, dtype in out],
        scratch_shapes=scratch,
        compiler_params=pltpu.CompilerParams(vmem_limit_bytes=VMEM_LIMIT),
        cost_estimate=pl.CostEstimate(flops=cost, bytes_accessed=1 << 16, transcendentals=0),
        name=name,
    )(*operands, *before)
    line[:] = [min(results, key=lambda x: x.size)]
    return results


def put_bit(i, position, value):
    low = i & ((1 << position) - 1)
    return ((i >> position) << (position + 1)) | (value << position) | low


def cut_copies(panel_ref, keep_ref, send_ref, panel, place, replica):
    groups, share, width = keep_ref.shape[2:]
    rank = pl.multiple_of(replica * share, share)
    copies = []
    for low, cut_ref in enumerate((keep_ref, keep_ref, send_ref, send_ref)):
        for high in range(groups):
            column = pl.multiple_of((place ^ (4 * high + low)) * width, width)
            copies.append(
                (panel_ref.at[0, pl.ds(rank, share), pl.ds(column, width)], cut_ref.at[low % 2, panel, high])
            )
    return copies


def run_copies(copies, sems):
    copies = [pltpu.make_async_copy(a, b, sems.at[i]) for i, (a, b) in enumerate(copies)]
    for copy in copies:
        copy.start()
    for copy in copies:
        copy.wait()


def pick_kernel(w_ref, shrink_ref, expand_ref, pick_ref, keep_ref, send_ref, sems):
    place, replica = lax.axis_index("tp"), lax.axis_index("rep")
    pairs, _, width = pick_ref.shape
    copies = []
    for i in range(pairs):
        column = pl.multiple_of((2 * (i ^ (place // 2)) + 1 - place % 2) * width, width)
        copies.append((w_ref.at[:, pl.ds(column, width)], pick_ref.at[i]))
    copies += cut_copies(shrink_ref, keep_ref, send_ref, 0, place, replica)
    copies += cut_copies(expand_ref, keep_ref, send_ref, 1, place, replica)
    run_copies(copies, sems)


def pick(line, weight, shrink_panels, expand_panels, size, replicas):
    depth, full = weight.shape
    pairs, width = size // 2, full // size
    cut = ((2, 2, size // 4, shrink_panels.shape[1] // replicas, width), BF16)
    return call(
        line,
        pick_kernel,
        "pick",
        (),
        (weight, shrink_panels, expand_panels),
        [((pairs, depth, width), BF16), cut, cut],
        0,
        scratch=[pltpu.SemaphoreType.DMA((pairs + 2 * size,))],
    )


def attention_kernel(
    lengths_ref, ids_ref, q_hbm, kc_hbm, vc_hbm, nk_hbm, nv_hbm, w_hbm,
    out_ref, own_ref,
    q_ref, kc_ref, vc_ref, nk_ref, nv_ref, q_sems, w_sems,
):
    place = lax.axis_index("tp")
    steps, requests, width = q_ref.shape
    heads = width // HD
    cached, fresh = kc_ref.shape[0], nk_ref.shape[0]
    block = own_ref.shape[2]
    size = 2 * own_ref.shape[0]
    group_heads = size * width // kc_hbm.shape[2]
    head = pl.multiple_of(place * heads // group_heads * HD, HD)
    parts = 2
    part = requests // parts
    loads = []
    for n in range(parts):
        span = pl.ds(n * part, part)
        pieces = [(q_hbm.at[:, span, :], q_ref.at[:, span, :])]
        for a, b in ((kc_hbm, kc_ref), (nk_hbm, nk_ref), (vc_hbm, vc_ref), (nv_hbm, nv_ref)):
            pieces.append((a.at[:, span, pl.ds(head, HD)], b.at[:, span, :]))
        loads.append([pltpu.make_async_copy(a, b, q_sems.at[n, i]) for i, (a, b) in enumerate(pieces)])
    pair, mine = place // 2, place % 2
    others = []
    for i in range(own_ref.shape[0]):
        column = pl.multiple_of((2 * (i ^ pair) + mine) * block, block)
        others.append((w_hbm.at[:, pl.ds(column, block)], own_ref.at[i]))
    others = [pltpu.make_async_copy(a, b, w_sems.at[i]) for i, (a, b) in enumerate(others)]
    for copy in [c for load in loads for c in load] + others:
        copy.start()

    group = GROUP_REQ
    rows, columns = steps * heads * group, (cached + fresh) * group
    row = lax.broadcasted_iota(jnp.int32, (rows, columns), 0)
    column = lax.broadcasted_iota(jnp.int32, (rows, columns), 1)
    same = row % group == column % group
    position = column // group
    step = row // (heads * group)
    fresh_ok = jnp.logical_and(position >= cached, position - cached <= step)
    column_position = lax.broadcasted_iota(jnp.int32, (1, columns), 1) // group
    tail = lax.broadcasted_iota(jnp.int32, (group, requests), 0) == 0
    out_ref[steps * requests :, :] = jnp.zeros((group, width), BF16)
    out_ref[steps * requests :, :requests] = jnp.where(tail, ids_ref[...].astype(F32), 0.0).astype(BF16)
    for n in range(parts):
        for copy in loads[n]:
            copy.wait()
        for i in range(n * part // group, (n + 1) * part // group):
            span = slice(i * group, (i + 1) * group)
            query = jnp.concatenate(
                [q_ref[s, span, h * HD : (h + 1) * HD] for s in range(steps) for h in range(heads)], 0
            )
            keys = jnp.concatenate(
                [kc_ref[p, span, :] for p in range(cached)] + [nk_ref[s, span, :] for s in range(fresh)], 0
            )
            values = jnp.concatenate(
                [vc_ref[p, span, :] for p in range(cached)] + [nv_ref[s, span, :] for s in range(fresh)], 0
            )
            scores = lax.dot_general(
                query, keys, (((1,), (1,)), ((), ())), preferred_element_type=F32
            ) * (1.0 / HD**0.5)
            limit = jnp.concatenate([lengths_ref[:, span]] * (cached + fresh), 1)
            cached_ok = column_position < limit
            visible = jnp.logical_and(same, jnp.logical_or(cached_ok, fresh_ok))
            scores = jnp.where(visible, scores, -1e30)
            scaled = jnp.exp(scores - scores.max(-1, keepdims=True))
            weights = (scaled / scaled.sum(-1, keepdims=True)).astype(BF16)
            mixed = jnp.dot(weights, values, preferred_element_type=F32).astype(BF16)
            for s in range(steps):
                for h in range(heads):
                    at = (s * heads + h) * group
                    to = s * requests + i * group
                    out_ref[to : to + group, h * HD : (h + 1) * HD] = mixed[at : at + group, :]
    for copy in others:
        copy.wait()


def attend(line, queries, key_cache, value_cache, new_keys, new_values, cache_lengths, adapter_ids, weight, size):
    steps, requests, width = queries.shape
    cached = key_cache.shape[1]
    depth, full = weight.shape
    block, pairs = full // size, size // 2
    return call(
        line,
        attention_kernel,
        "attention",
        (cache_lengths.reshape(1, -1), adapter_ids.reshape(1, -1)),
        (queries, key_cache.transpose(1, 0, 2), value_cache.transpose(1, 0, 2), new_keys, new_values, weight),
        [
            ((steps * requests + GROUP_REQ, width), BF16),
            ((pairs, depth, block), BF16),
        ],
        4 * requests * steps * width * (cached + steps) * GROUP_REQ,
        [
            pltpu.VMEM((steps, requests, width), BF16),
            pltpu.VMEM((cached, requests, HD), BF16),
            pltpu.VMEM((cached, requests, HD), BF16),
            pltpu.VMEM((steps, requests, HD), BF16),
            pltpu.VMEM((steps, requests, HD), BF16),
            pltpu.SemaphoreType.DMA((2, 5)),
            pltpu.SemaphoreType.DMA((pairs,)),
        ],
    )


def product(span, which, a_ref, b_ref, own_ref, other_ref):
    return jnp.dot(a_ref[span, :], own_ref[which], preferred_element_type=F32) + jnp.dot(
        b_ref[span, :], other_ref[which], preferred_element_type=F32
    )


def far_kernel(span, stage, *refs):
    operands, out_ref = refs[:-1], refs[-1]
    for i in range(out_ref.shape[0]):
        out_ref[i] = product(span, put_bit(i, stage, 1), *operands).astype(BF16)


def near_kernel(span, stage, following, *refs):
    operands, (arrived_ref, keep_ref, send_ref) = refs[:-3], refs[-3:]
    for i in range(keep_ref.shape[0]):
        for value, out_ref in ((1, send_ref), (0, keep_ref)):
            at = put_bit(i, following, value)
            total = product(span, put_bit(at, stage, 0), *operands) + arrived_ref[at].astype(F32)
            out_ref[i] = total.astype(out_ref.dtype)


def near_all_kernel(span, stage, *refs):
    operands, arrived_ref, out_refs = refs[:4], refs[4], refs[5:]
    for i, out_ref in enumerate(out_refs):
        total = product(span, put_bit(i, stage, 0), *operands) + arrived_ref[i].astype(F32)
        out_ref[0] = total.astype(out_ref.dtype)


def near_all(line, span, stage, operands, arrived):
    pairs, depth, width = operands[2].shape
    rows = span.stop - span.start
    return call(
        line,
        functools.partial(near_all_kernel, span, stage),
        "near",
        (*operands, arrived),
        (),
        [((1, rows, width), F32)] + [((1, rows, width), BF16)] * (pairs // 2 - 1),
        2 * rows * depth * pairs * width,
    )


def far(line, span, stage, operands, after=()):
    pairs, depth, width = operands[2].shape
    rows = span.stop - span.start
    return call(
        line,
        functools.partial(far_kernel, span, stage),
        "far",
        operands,
        (),
        [((pairs // 2, rows, width), BF16)],
        2 * rows * depth * pairs * width,
        after=after,
    )[0]


def near(line, span, stage, following, operands, arrived, after=()):
    pairs, depth, width = operands[2].shape
    rows = span.stop - span.start
    return call(
        line,
        functools.partial(near_kernel, span, stage, following),
        "near",
        (*operands, arrived),
        (),
        [((pairs // 4, rows, width), F32), ((pairs // 4, rows, width), BF16)],
        2 * rows * depth * pairs * width,
        after=after,
    )


def add_kernel(following, keep_ref, arrived_ref, more_ref, send_ref):
    for i in range(more_ref.shape[0]):
        for value, out_ref in ((1, send_ref), (0, more_ref)):
            at = put_bit(i, following, value)
            out_ref[i] = (keep_ref[at] + arrived_ref[at].astype(F32)).astype(out_ref.dtype)


def add(line, following, keep, arrived):
    shape = (keep.shape[0] // 2,) + keep.shape[1:]
    return call(
        line,
        functools.partial(add_kernel, following),
        "add",
        (keep, arrived),
        (),
        [(shape, F32), (shape, BF16)],
        2 * keep.size,
    )


def total_kernel(a_ref, b_ref, out_ref):
    out_ref[...] = a_ref[...] + b_ref[...]


def total(line, a, b):
    return call(line, total_kernel, "total", (a, b), (), [(a.shape, a.dtype)], a.size)[0]


def side_kernel(keep_ref, arrived_ref, more_ref, send_ref):
    for source, ref in enumerate((keep_ref, arrived_ref)):
        more_ref[source] = ref[0]
        send_ref[source] = ref[1]


def side(line, keep, arrived, after):
    out = (keep.shape, BF16)
    return call(line, side_kernel, "side", (keep, arrived), (), [out, out], 0, after=after)


def sort_kernel(keep_ref, arrived_ref, *out_refs):
    for high, out_ref in enumerate(out_refs):
        for core, ref in enumerate((keep_ref, arrived_ref)):
            for side in range(2):
                for panel in range(2):
                    out_ref[panel, 2 * side + core] = ref[side, panel, high]


def sort(line, keep, arrived, after):
    groups, share, width = keep.shape[2:]
    return call(line, sort_kernel, "sort", (keep, arrived), (), [((2, 4, share, width), BF16)] * groups, 0, after=after)


def far_blocks(blocks):
    size = 4 * len(blocks)
    return [blocks[0]] + [swap(b, "tp", 4 * h, size) for h, b in enumerate(blocks) if h]


def expanding_kernel(*refs):
    out_ref = refs[-1]
    for high, ref in enumerate(refs[:-1]):
        for source in range(4):
            out_ref[4 * high + source] = ref[1, source]


def expanding(line, blocks):
    share, width = blocks[0].shape[2:]
    out = [((4 * len(blocks), share, width), BF16)]
    return call(line, expanding_kernel, "expanding", blocks, (), out, 0)[0]


def owners(ids, shape, high, share):
    owner = 4 * high + lax.broadcasted_iota(jnp.int32, shape, 1) // share
    return owner == (ids ^ lax.axis_index("tp"))


def shrink_kernel(steps, groups, *refs):
    panels, attended, out_ref = refs[:groups], refs[groups:-1], refs[-1]
    share, width = panels[0].shape[2:]
    for k, a_ref in enumerate(attended):
        rows = a_ref.shape[0] - GROUP_REQ
        requests = rows // steps
        row = lax.broadcasted_iota(jnp.int32, (requests, requests), 0)
        column = lax.broadcasted_iota(jnp.int32, (requests, requests), 1)
        line = a_ref[rows : rows + GROUP_REQ, :requests].astype(F32)[:1, :]
        ids = jnp.where(row == column, line, 0.0).sum(1, keepdims=True).astype(jnp.int32)
        ids = jnp.concatenate([ids] * steps, 0)
        total = None
        for high, panel in enumerate(panels):
            flat = panel[0].reshape(4 * share, width)
            ranks = lax.dot_general(
                a_ref[:rows, :], flat, (((1,), (1,)), ((), ())), preferred_element_type=F32
            )
            ranks = jnp.where(owners(ids, ranks.shape, high, share), ranks, 0.0)
            total = ranks if total is None else total + ranks
        part = total[:, :share]
        for i in range(1, 4):
            part = part + total[:, share * i : share * (i + 1)]
        fold = out_ref.shape[1]
        out_ref[k] = jnp.concatenate([part[i * fold : (i + 1) * fold] for i in range(rows // fold)], 1)


def shrink(line, steps, panels, attended):
    replicas, rows, share = len(attended), attended[0].shape[0] - GROUP_REQ, panels[0].shape[2]
    return call(
        line,
        functools.partial(shrink_kernel, steps, len(panels)),
        "shrink",
        (*panels, *attended),
        (),
        [((replicas, rows * share // LANES, LANES), F32)],
        2 * rows * replicas * len(panels) * panels[0].size,
    )[0]


def expand_kernel(steps, replicas, ids_ref, *refs):
    ranks, panels, out_ref = refs[:replicas], refs[replicas:-1], refs[-1]
    _, share, width = panels[0].shape
    ids = jnp.concatenate([ids_ref[...]] * steps, 0)
    total = None
    for k, rank_ref in enumerate(ranks):
        folded = rank_ref[0].astype(BF16).astype(F32)
        part = jnp.concatenate([folded[:, i * share : (i + 1) * share] for i in range(LANES // share)], 0)
        part = jnp.concatenate([part] * 4, 1)
        panel = panels[k]
        spread = [
            jnp.where(owners(ids, part.shape, high, share), part, 0.0).astype(BF16)
            for high in range(panel.shape[0] // 4)
        ]
        term = jnp.dot(
            jnp.concatenate(spread, 1), panel[...].reshape(-1, width), preferred_element_type=F32
        )
        total = term if total is None else total + term
    out_ref[...] = total


def expand(line, steps, ids, ranks, panels):
    rows, width = steps * ids.shape[0], panels[0].shape[2]
    return call(
        line,
        functools.partial(expand_kernel, steps, len(ranks)),
        "expand",
        (ids, *ranks, *panels),
        (),
        [((rows, width), F32)],
        2 * rows * len(panels) * panels[0].size,
    )[0]


def fold_kernel(*refs):
    total = refs[0][0]
    for ref in refs[1:-1]:
        total = total + ref[0].astype(F32)
    refs[-1][...] = total


def fold(line, terms):
    return call(line, fold_kernel, "fold", terms, (), [(terms[0].shape[1:], F32)], 0)[0]


def finish_kernel(spans, lora_ref, *refs):
    refs, out_ref = refs[:-1], refs[-1]
    for n, span in enumerate(spans[:-1]):
        out_ref[span, :] = (refs[n][...] + lora_ref[span, :]).astype(BF16)
    total = lora_ref[spans[-1], :]
    for ref in refs[len(spans) - 1 :]:
        total = total + ref[0].astype(F32)
    out_ref[spans[-1], :] = total.astype(BF16)


def finish(spans, lora, sums, terms):
    operands = [pltpu.with_memory_space_constraint(x, pltpu.VMEM) for x in (lora, *sums, *terms)]
    return pl.pallas_call(
        functools.partial(finish_kernel, spans),
        in_specs=[pl.BlockSpec(memory_space=pltpu.VMEM)] * len(operands),
        out_specs=pl.BlockSpec(memory_space=pltpu.VMEM),
        out_shape=jax.ShapeDtypeStruct(lora.shape, BF16),
        compiler_params=pltpu.CompilerParams(vmem_limit_bytes=VMEM_LIMIT),
        cost_estimate=pl.CostEstimate(flops=4 * lora.size, bytes_accessed=1 << 20, transcendentals=0),
        name="finish",
    )(*operands)


def swap(array, axis, bit, size):
    return lax.ppermute(array, axis, [(i, i ^ bit) for i in range(size)])


def body(
    size,
    replicas,
    queries,
    key_cache,
    value_cache,
    new_keys,
    new_values,
    cache_lengths,
    adapter_ids,
    out_weight,
    shrink_panels,
    expand_panels,
):
    steps, requests, local = queries.shape
    rows = steps * requests
    pairs = size // 2
    stages = size.bit_length() - 2
    plan = SMALL_PLAN if stages == 3 else ((16, tuple(range(stages))),)
    spans, first = [], 0
    for part, _ in plan:
        spans.append(slice(first, first + rows * part // 16))
        first += rows * part // 16

    line = []
    last = len(plan) - 1
    keeps, sends, cames, sums = {}, {}, {}, {}

    def begin(n, after=()):
        order = plan[n][1]
        sends[n] = far(line, spans[n], order[0], operands, after)
        cames[n] = swap(sends[n], "tp", 2 << order[0], size)

    def middle(n, after=()):
        order = plan[n][1]
        if len(order) == 1:
            keep, *rest = near_all(line, spans[n], order[0], operands, cames[n])
            sums[n] = [keep] + [swap(x, "tp", 4 * (h + 1), size) for h, x in enumerate(rest)]
            return
        following = order[1] - (order[1] > order[0])
        keeps[n], send = near(line, spans[n], order[0], following, operands, cames[n], after)
        cames[n] = swap(send, "tp", 2 << order[1], size)

    def end(n):
        order = plan[n][1]
        for i in range(2, len(order)):
            left = order[i] - sum(order[i] > t for t in order[:i])
            keeps[n], send = add(line, left, keeps[n], cames[n])
            cames[n] = swap(send, "tp", 2 << order[i], size)
        if n not in sums:
            sums[n] = [keeps[n], cames[n]]

    picked, cut_keep, cut_send = pick(line, out_weight, shrink_panels, expand_panels, size, replicas)
    weight_other = swap(picked, "tp", 1, size)
    cut_came = swap(cut_send, "tp", 2, size)
    attended, weight_own = attend(
        line, queries, key_cache, value_cache, new_keys, new_values, cache_lengths, adapter_ids, out_weight, size
    )
    attended_other = swap(attended, "tp", 1, size)
    attended_all = [attended] + [swap(attended, "rep", k, replicas) for k in range(1, replicas)]
    operands = (attended, attended_other, weight_own, weight_other)

    begin(0)
    if last:
        begin(2)
    side_keep, side_send = side(line, cut_keep, cut_came, [cames[2]] if last else ())
    panels = far_blocks(sort(line, side_keep, swap(side_send, "tp", 1, size), ()))
    if last:
        begin(1, attended_all[1:])
    shrunk = shrink(line, steps, panels, attended_all)
    came = swap(shrunk, "tp", 2, size)
    middle(0)
    expanding_all = [expanding(line, panels)]
    expanding_all += [swap(expanding_all[0], "rep", k, replicas) for k in range(1, replicas)]
    if last:
        middle(2)
    shrunk = total(line, shrunk, came)
    came = swap(shrunk, "tp", 4, size)
    end(0)
    if last:
        middle(1)
    for bit in range(3, stages + 1):
        shrunk = total(line, shrunk, came)
        came = swap(shrunk, "tp", 1 << bit, size)
    if last:
        sums[0] = [fold(line, sums[0])]
        end(2)
    shrunk = total(line, shrunk, came)
    came = swap(shrunk, "tp", 1, size)
    if last:
        end(1)
    shrunk = total(line, shrunk, came)
    ranks = [shrunk[:1]] + [swap(shrunk[k : k + 1], "rep", k, replicas) for k in range(1, replicas)]
    lora = expand(line, steps, adapter_ids, ranks, expanding_all)
    if last:
        sums[2] = [fold(line, sums[2])]
    ready = [n for n in (0, 2) if n < last or n == 2 and last]
    spans = [spans[n] for n in (*ready, 1 if last else 0)]
    ready = [sums[n][0] for n in ready]
    last = 1 if last else 0
    return finish(spans, lora, ready, sums[last]).reshape(queries.shape)


def solution(mesh):
    return jax.shard_map(
        functools.partial(body, mesh.shape["tp"], mesh.shape["rep"]),
        mesh=mesh,
        in_specs=(
            P(None, "rep", "tp"),
            P("rep", None, None),
            P("rep", None, None),
            P(None, "rep", None),
            P(None, "rep", None),
            P("rep"),
            P("rep", None),
            P("tp", None),
            P("tp", None, None),
            P("tp", None, None),
        ),
        out_specs=P(None, "rep", "tp"),
        check_vma=False,
    )
```

```python
import functools

import jax
import jax.numpy as jnp
from jax import lax
from jax.experimental import pallas as pl
from jax.experimental.pallas import tpu as pltpu
from jax.sharding import PartitionSpec as P

HD = 128
LANES = 128
GROUP_REQ = 16
VMEM_LIMIT = 24 << 20
F32 = jnp.float32
BF16 = jnp.bfloat16
PLAN = ((7, (0, 1, 2)), (5, (0, 1, 2)), (1, (0, 1, 2)), (3, (1, 0, 2)))
FIRST_PIECE = 1
RIDE = 2
STEPS = ('far3', 'far0', 'side', 'have3', 'sort', 'have_x', 'far1', 'near0', 'shrink', 'core', 'far2', 'expanding', 'near3', 'near1', 'end0', 'near2', 'end1', 'fold0', 'end3', 'end2', 'fold1', 'ranks', 'expand', 'fold3')
PLAIN_STEPS = ("side", "sort", "shrink", "core", "far0", "near0", "end0", "ranks", "expanding", "expand")
COST = 1


def call(line, kernel, name, vmem, hbm, out, cost, scratch=(), after=()):
    operands = [pltpu.with_memory_space_constraint(x, pltpu.VMEM) for x in vmem]
    operands += [pltpu.with_memory_space_constraint(x, pltpu.HBM) for x in hbm]
    before = [*line, *after]
    count, extra = len(operands), len(before)

    def run(*refs):
        kernel(*refs[:count], *refs[count + extra :])

    results = pl.pallas_call(
        run,
        in_specs=[pl.BlockSpec(memory_space=pltpu.VMEM)] * len(vmem)
        + [pl.BlockSpec(memory_space=pltpu.HBM)] * len(hbm)
        + [pl.BlockSpec(memory_space=pl.ANY)] * extra,
        out_specs=[pl.BlockSpec(memory_space=pltpu.VMEM)] * len(out),
        out_shape=[pltpu.VMEM(shape, dtype) for shape, dtype in out],
        scratch_shapes=scratch,
        compiler_params=pltpu.CompilerParams(vmem_limit_bytes=VMEM_LIMIT),
        cost_estimate=pl.CostEstimate(flops=COST * cost, bytes_accessed=1 << 16, transcendentals=0),
        name=name,
    )(*operands, *before)
    line[:] = [min(results, key=lambda x: x.size)]
    return results


def put_bit(i, position, value):
    low = i & ((1 << position) - 1)
    return ((i >> position) << (position + 1)) | (value << position) | low


def cut_copies(panel_ref, keep_ref, send_ref, panel, place, replica):
    groups, share, width = keep_ref.shape[2:]
    rank = pl.multiple_of(replica * share, share)
    copies = []
    for low, cut_ref in enumerate((keep_ref, keep_ref, send_ref, send_ref)):
        for high in range(groups):
            column = pl.multiple_of((place ^ (4 * high + low)) * width, width)
            copies.append(
                (panel_ref.at[0, pl.ds(rank, share), pl.ds(column, width)], cut_ref.at[low % 2, panel, high])
            )
    return copies


def run_copies(copies, sems):
    copies = [pltpu.make_async_copy(a, b, sems.at[i]) for i, (a, b) in enumerate(copies)]
    for copy in copies:
        copy.start()
    for copy in copies:
        copy.wait()


def cut_kernel(shrink_ref, expand_ref, keep_ref, send_ref, sems):
    place, replica = lax.axis_index("tp"), lax.axis_index("rep")
    copies = cut_copies(shrink_ref, keep_ref, send_ref, 0, place, replica)
    run_copies(copies + cut_copies(expand_ref, keep_ref, send_ref, 1, place, replica), sems)


def cut(line, shrink_panels, expand_panels, size, replicas):
    out = ((2, 2, size // 4, shrink_panels.shape[1] // replicas, shrink_panels.shape[2] // size), BF16)
    return call(
        line,
        cut_kernel,
        "cut",
        (),
        (shrink_panels, expand_panels),
        [out, out],
        0,
        scratch=[pltpu.SemaphoreType.DMA((2 * size,))],
    )


def attention_kernel(
    lengths_ref, ids_ref, q_hbm, kc_hbm, vc_hbm, nk_hbm, nv_hbm, w_hbm, out_ref, own_ref, other_ref, *rest
):
    *piece_refs, q_ref, kc_ref, vc_ref, nk_ref, nv_ref, q_sems, w_sems = rest
    place = lax.axis_index("tp")
    steps, requests, width = q_ref.shape
    heads = width // HD
    cached, fresh = kc_ref.shape[0], nk_ref.shape[0]
    block = own_ref.shape[2]
    size = 2 * own_ref.shape[0]
    group_heads = size * width // kc_hbm.shape[2]
    head = pl.multiple_of(place * heads // group_heads * HD, HD)
    parts = 2
    part = requests // parts
    loads = []
    for n in range(parts):
        span = pl.ds(n * part, part)
        pieces = [(q_hbm.at[:, span, :], q_ref.at[:, span, :])]
        for a, b in ((kc_hbm, kc_ref), (nk_hbm, nk_ref), (vc_hbm, vc_ref), (nv_hbm, nv_ref)):
            pieces.append((a.at[:, span, pl.ds(head, HD)], b.at[:, span, :]))
        loads.append([pltpu.make_async_copy(a, b, q_sems.at[n, i]) for i, (a, b) in enumerate(pieces)])
    pair, mine = place // 2, place % 2
    others = []
    for ref, core in ((other_ref, 1 - mine), (own_ref, mine)):
        for i in range(ref.shape[0]):
            column = pl.multiple_of((2 * (i ^ pair) + core) * block, block)
            others.append((w_hbm.at[:, pl.ds(column, block)], ref.at[i]))
    others = [pltpu.make_async_copy(a, b, w_sems.at[i]) for i, (a, b) in enumerate(others)]
    for copy in [c for load in loads for c in load] + others:
        copy.start()

    group = GROUP_REQ
    rows, columns = steps * heads * group, (cached + fresh) * group
    row = lax.broadcasted_iota(jnp.int32, (rows, columns), 0)
    column = lax.broadcasted_iota(jnp.int32, (rows, columns), 1)
    same = row % group == column % group
    position = column // group
    step = row // (heads * group)
    fresh_ok = jnp.logical_and(position >= cached, position - cached <= step)
    column_position = lax.broadcasted_iota(jnp.int32, (1, columns), 1) // group
    tail = lax.broadcasted_iota(jnp.int32, (group, requests), 0) == 0
    out_ref[steps * requests :, :] = jnp.zeros((group, width), BF16)
    out_ref[steps * requests :, :requests] = jnp.where(tail, ids_ref[...].astype(F32), 0.0).astype(BF16)
    for n in range(parts):
        for copy in loads[n]:
            copy.wait()
        for i in range(n * part // group, (n + 1) * part // group):
            span = slice(i * group, (i + 1) * group)
            query = jnp.concatenate(
                [q_ref[s, span, h * HD : (h + 1) * HD] for s in range(steps) for h in range(heads)], 0
            )
            keys = jnp.concatenate(
                [kc_ref[p, span, :] for p in range(cached)] + [nk_ref[s, span, :] for s in range(fresh)], 0
            )
            values = jnp.concatenate(
                [vc_ref[p, span, :] for p in range(cached)] + [nv_ref[s, span, :] for s in range(fresh)], 0
            )
            scores = lax.dot_general(
                query, keys, (((1,), (1,)), ((), ())), preferred_element_type=F32
            ) * (1.0 / HD**0.5)
            limit = jnp.concatenate([lengths_ref[:, span]] * (cached + fresh), 1)
            cached_ok = column_position < limit
            visible = jnp.logical_and(same, jnp.logical_or(cached_ok, fresh_ok))
            scores = jnp.where(visible, scores, -1e30)
            scaled = jnp.exp(scores - scores.max(-1, keepdims=True))
            weights = (scaled / scaled.sum(-1, keepdims=True)).astype(BF16)
            mixed = jnp.dot(weights, values, preferred_element_type=F32).astype(BF16)
            for s in range(steps):
                for h in range(heads):
                    at = (s * heads + h) * group
                    to = s * requests + i * group
                    out_ref[to : to + group, h * HD : (h + 1) * HD] = mixed[at : at + group, :]
    first = 0
    for piece_ref in piece_refs:
        piece_ref[...] = out_ref[first : first + piece_ref.shape[0], :]
        first += piece_ref.shape[0]
    for copy in others:
        copy.wait()


def attend(line, queries, key_cache, value_cache, new_keys, new_values, cache_lengths, adapter_ids, weight, size, pieces):
    steps, requests, width = queries.shape
    cached = key_cache.shape[1]
    depth, full = weight.shape
    block, pairs = full // size, size // 2
    return call(
        line,
        attention_kernel,
        "attention",
        (cache_lengths.reshape(1, -1), adapter_ids.reshape(1, -1)),
        (queries, key_cache.transpose(1, 0, 2), value_cache.transpose(1, 0, 2), new_keys, new_values, weight),
        [
            ((steps * requests + GROUP_REQ, width), BF16),
            ((pairs, depth, block), BF16),
            ((pairs, depth, block), BF16),
        ]
        + [((piece, width), BF16) for piece in pieces],
        4 * requests * steps * width * (cached + steps) * GROUP_REQ,
        [
            pltpu.VMEM((steps, requests, width), BF16),
            pltpu.VMEM((cached, requests, HD), BF16),
            pltpu.VMEM((cached, requests, HD), BF16),
            pltpu.VMEM((steps, requests, HD), BF16),
            pltpu.VMEM((steps, requests, HD), BF16),
            pltpu.SemaphoreType.DMA((2, 5)),
            pltpu.SemaphoreType.DMA((2 * pairs,)),
        ],
    )


def product(spans, which, a_ref, b_ref, own_ref, other_ref):
    return jnp.dot(a_ref[spans[0], :], own_ref[which], preferred_element_type=F32) + jnp.dot(
        b_ref[spans[1], :], other_ref[which], preferred_element_type=F32
    )


def pack(small, blocks, width):
    part = small.shape[0] // blocks
    fold = part * LANES // width
    return [
        jnp.concatenate([small[i * part + j : i * part + j + fold] for j in range(0, part, fold)], 1)
        for i in range(blocks)
    ]


def unpack(blocks):
    return jnp.concatenate(
        [block[:, j : j + LANES] for block in blocks for j in range(0, block.shape[1], LANES)], 0
    )


def extra_rows(small, blocks, width):
    return 0 if small is None else small.size // (blocks * width)


def pass_small(small_ref, arrived_ref, more_ref, send_ref, rows):
    flat = small_ref[...].reshape(-1, LANES)
    flat = flat + unpack([arrived_ref[i, rows:, :].astype(F32) for i in range(arrived_ref.shape[0])])
    more_ref[...] = flat.reshape(more_ref.shape)
    if send_ref is not None:
        for i, block in enumerate(pack(flat.astype(BF16), send_ref.shape[0], send_ref.shape[2])):
            send_ref[i, rows:, :] = block


def far_kernel(spans, stage, *refs):
    operands, sent_refs, out_ref = refs[:4], refs[4:-1], refs[-1]
    rows = spans[0].stop - spans[0].start
    for i in range(out_ref.shape[0]):
        out_ref[i, :rows, :] = product(spans, put_bit(i, stage, 1), *operands).astype(BF16)
    for sent_ref in sent_refs:
        for i, block in enumerate(pack(sent_ref[...].reshape(-1, LANES), out_ref.shape[0], out_ref.shape[2])):
            out_ref[i, rows:, :] = block


def far(line, spans, stage, operands, sent=None):
    pairs, depth, width = operands[2].shape
    rows = spans[0].stop - spans[0].start
    more = extra_rows(sent, pairs // 2, width)
    return call(
        line,
        functools.partial(far_kernel, spans, stage),
        "far",
        operands if sent is None else (*operands, sent),
        (),
        [((pairs // 2, rows + more, width), BF16)],
        2 * rows * depth * pairs * width,
    )[0]


def near_kernel(spans, stage, following, *refs):
    operands, arrived_ref, refs = refs[:4], refs[4], refs[5:]
    rows = spans[0].stop - spans[0].start
    keep_ref, send_ref = refs[-2:]
    for i in range(keep_ref.shape[0]):
        for value, out_ref in ((1, send_ref), (0, keep_ref)):
            at = put_bit(i, following, value)
            total = product(spans, put_bit(at, stage, 0), *operands) + arrived_ref[at, :rows, :].astype(F32)
            out_ref[i, :rows, :] = total.astype(out_ref.dtype)
    if len(refs) > 2:
        pass_small(refs[0], arrived_ref, refs[1], send_ref, rows)


def near(line, spans, stage, following, operands, arrived, small=None):
    pairs, depth, width = operands[2].shape
    rows = spans[0].stop - spans[0].start
    more = extra_rows(small, pairs // 4, width)
    return call(
        line,
        functools.partial(near_kernel, spans, stage, following),
        "near",
        (*operands, arrived) if small is None else (*operands, arrived, small),
        (),
        ([] if small is None else [(small.shape, F32)])
        + [((pairs // 4, rows, width), F32), ((pairs // 4, rows + more, width), BF16)],
        2 * rows * depth * pairs * width,
    )


def add_kernel(following, keep_ref, arrived_ref, *refs):
    more_ref, send_ref = refs[-2:]
    rows = keep_ref.shape[1]
    for i in range(more_ref.shape[0]):
        for value, out_ref in ((1, send_ref), (0, more_ref)):
            at = put_bit(i, following, value)
            total = keep_ref[at] + arrived_ref[at, :rows, :].astype(F32)
            out_ref[i, :rows, :] = total.astype(out_ref.dtype)
    if len(refs) > 2:
        pass_small(refs[0], arrived_ref, refs[1], send_ref, rows)


def add(line, following, keep, arrived, small=None):
    blocks, rows, width = keep.shape
    more = extra_rows(small, blocks // 2, width)
    return call(
        line,
        functools.partial(add_kernel, following),
        "add",
        (keep, arrived) if small is None else (keep, arrived, small),
        (),
        ([] if small is None else [(small.shape, F32)])
        + [((blocks // 2, rows, width), F32), ((blocks // 2, rows + more, width), BF16)],
        2 * keep.size,
    )


def total_kernel(a_ref, b_ref, *out_refs):
    for out_ref in out_refs:
        out_ref[...] = (a_ref[...] + b_ref[...].astype(F32)).astype(out_ref.dtype)


def total(line, a, b):
    return call(line, total_kernel, "total", (a, b), (), [(a.shape, F32), (a.shape, BF16)], a.size)


def arrive_kernel(rows, small_ref, arrived_ref, *out_refs):
    flat = small_ref[...].reshape(-1, LANES) + unpack([arrived_ref[0, rows:, :].astype(F32)])
    small = flat.reshape(small_ref.shape).astype(BF16)
    for k, out_ref in enumerate(out_refs):
        out_ref[...] = small[k]


def arrive(line, rows, small, arrived):
    out = [(small.shape[1:], BF16)] * small.shape[0]
    return call(line, functools.partial(arrive_kernel, rows), "arrive", (small, arrived), (), out, 0)


def side_kernel(keep_ref, arrived_ref, more_ref, *send_refs):
    for source, ref in enumerate((keep_ref, arrived_ref)):
        more_ref[source] = ref[0]
        for panel, send_ref in enumerate(send_refs):
            send_ref[source] = ref[1, panel]


def side(line, keep, arrived, after):
    part = (keep.shape[:1] + keep.shape[2:], BF16)
    return call(line, side_kernel, "side", (keep, arrived), (), [(keep.shape, BF16), part, part], 0, after=after)


def sort_kernel(keep_ref, *refs):
    arrived_refs, out_refs = refs[:2], refs[2:]
    for high, out_ref in enumerate(out_refs):
        for side in range(2):
            for panel in range(2):
                out_ref[panel, 2 * side] = keep_ref[side, panel, high]
                out_ref[panel, 2 * side + 1] = arrived_refs[panel][side, high]


def sort(line, keep, arrived):
    groups, share, width = keep.shape[2:]
    return call(line, sort_kernel, "sort", (keep, *arrived), (), [((2, 4, share, width), BF16)] * groups, 0)


def far_blocks(blocks):
    size = 4 * len(blocks)
    return [blocks[0]] + [swap(b, "tp", 4 * h, size) for h, b in enumerate(blocks) if h]


def expanding_kernel(*refs):
    out_ref = refs[-1]
    for high, ref in enumerate(refs[:-1]):
        for source in range(4):
            out_ref[4 * high + source] = ref[1, source]


def expanding(line, blocks):
    share, width = blocks[0].shape[2:]
    out = [((4 * len(blocks), share, width), BF16)]
    return call(line, expanding_kernel, "expanding", blocks, (), out, 0)[0]


def owners(ids, shape, high, share):
    owner = 4 * high + lax.broadcasted_iota(jnp.int32, shape, 1) // share
    return owner == (ids ^ lax.axis_index("tp"))


def shrink_kernel(steps, groups, *refs):
    panels, attended, out_refs = refs[:groups], refs[groups:-2], refs[-2:]
    share, width = panels[0].shape[2:]
    for k, a_ref in enumerate(attended):
        rows = a_ref.shape[0] - GROUP_REQ
        requests = rows // steps
        row = lax.broadcasted_iota(jnp.int32, (requests, requests), 0)
        column = lax.broadcasted_iota(jnp.int32, (requests, requests), 1)
        line = a_ref[rows : rows + GROUP_REQ, :requests].astype(F32)[:1, :]
        ids = jnp.where(row == column, line, 0.0).sum(1, keepdims=True).astype(jnp.int32)
        ids = jnp.concatenate([ids] * steps, 0)
        total = None
        for high, panel in enumerate(panels):
            flat = panel[0].reshape(4 * share, width)
            ranks = lax.dot_general(
                a_ref[:rows, :], flat, (((1,), (1,)), ((), ())), preferred_element_type=F32
            )
            ranks = jnp.where(owners(ids, ranks.shape, high, share), ranks, 0.0)
            total = ranks if total is None else total + ranks
        part = total[:, :share]
        for i in range(1, 4):
            part = part + total[:, share * i : share * (i + 1)]
        fold = out_refs[0].shape[1]
        part = jnp.concatenate([part[i * fold : (i + 1) * fold] for i in range(rows // fold)], 1)
        for out_ref in out_refs:
            out_ref[k] = part.astype(out_ref.dtype)


def shrink(line, steps, panels, attended):
    replicas, rows, share = len(attended), attended[0].shape[0] - GROUP_REQ, panels[0].shape[2]
    return call(
        line,
        functools.partial(shrink_kernel, steps, len(panels)),
        "shrink",
        (*panels, *attended),
        (),
        [((replicas, rows * share // LANES, LANES), dtype) for dtype in (F32, BF16)],
        2 * rows * replicas * len(panels) * panels[0].size,
    )


def expand_kernel(steps, replicas, ids_ref, *refs):
    ranks, panels, out_ref = refs[:replicas], refs[replicas:-1], refs[-1]
    _, share, width = panels[0].shape
    ids = jnp.concatenate([ids_ref[...]] * steps, 0)
    total = None
    for k, rank_ref in enumerate(ranks):
        folded = rank_ref[...].astype(F32)
        part = jnp.concatenate([folded[:, i * share : (i + 1) * share] for i in range(LANES // share)], 0)
        part = jnp.concatenate([part] * 4, 1)
        panel = panels[k]
        spread = [
            jnp.where(owners(ids, part.shape, high, share), part, 0.0).astype(BF16)
            for high in range(panel.shape[0] // 4)
        ]
        term = jnp.dot(
            jnp.concatenate(spread, 1), panel[...].reshape(-1, width), preferred_element_type=F32
        )
        total = term if total is None else total + term
    out_ref[...] = total


def expand(line, steps, ids, ranks, panels):
    rows, width = steps * ids.shape[0], panels[0].shape[2]
    return call(
        line,
        functools.partial(expand_kernel, steps, len(ranks)),
        "expand",
        (ids, *ranks, *panels),
        (),
        [((rows, width), F32)],
        2 * rows * len(panels) * panels[0].size,
    )[0]


def fold_kernel(keep_ref, arrived_ref, out_ref):
    out_ref[...] = keep_ref[0] + arrived_ref[0, : keep_ref.shape[1], :].astype(F32)


def fold(line, terms):
    return call(line, fold_kernel, "fold", terms, (), [(terms[0].shape[1:], F32)], 0)[0]


def finish_kernel(spans, folded, lora_ref, *refs):
    refs, out_ref = refs[:-1], refs[-1]
    for n, span in enumerate(spans):
        if n < folded:
            total = refs[n][...]
        else:
            keep_ref, arrived_ref = refs[2 * n - folded : 2 * n - folded + 2]
            total = keep_ref[0] + arrived_ref[0, : keep_ref.shape[1], :].astype(F32)
        out_ref[span, :] = (total + lora_ref[span, :]).astype(BF16)


def finish(spans, lora, sums, terms):
    operands = [pltpu.with_memory_space_constraint(x, pltpu.VMEM) for x in (lora, *sums, *terms)]
    return pl.pallas_call(
        functools.partial(finish_kernel, spans, len(sums)),
        in_specs=[pl.BlockSpec(memory_space=pltpu.VMEM)] * len(operands),
        out_specs=pl.BlockSpec(memory_space=pltpu.VMEM),
        out_shape=jax.ShapeDtypeStruct(lora.shape, BF16),
        compiler_params=pltpu.CompilerParams(vmem_limit_bytes=VMEM_LIMIT),
        cost_estimate=pl.CostEstimate(flops=4 * lora.size, bytes_accessed=1 << 20, transcendentals=0),
        name="finish",
    )(*operands)


def swap(array, axis, bit, size):
    return lax.ppermute(array, axis, [(i, i ^ bit) for i in range(size)])


def body(
    size,
    replicas,
    queries,
    key_cache,
    value_cache,
    new_keys,
    new_values,
    cache_lengths,
    adapter_ids,
    out_weight,
    shrink_panels,
    expand_panels,
):
    steps, requests, local = queries.shape
    rows = steps * requests
    pairs = size // 2
    stages = size.bit_length() - 2
    if stages == 3:
        plan, first_piece, ride, steps_list = PLAN, FIRST_PIECE, RIDE, STEPS
    else:
        plan, first_piece, ride, steps_list = ((16, tuple(range(stages))),), 1, 0, PLAIN_STEPS
    spans, first = [], 0
    for part, _ in plan:
        spans.append(slice(first, first + rows * part // 16))
        first += rows * part // 16

    line = []
    last = len(plan) - 1
    keeps, cames, sums = {}, {}, {}

    def chunk(n):
        piece = 0 if n < first_piece else 1
        start = spans[first_piece].start if piece else 0
        there = slice(spans[n].start - start, spans[n].stop - start)
        return (spans[n], there), (attended, attended_other[piece], weight_own, weight_other)

    def begin(n):
        rows, operands = chunk(n)
        order = plan[n][1]
        block = far(line, rows, order[0], operands, sent if n == ride else None)
        cames[n] = swap(block, "tp", 2 << order[0], size)

    def middle(n):
        nonlocal shrunk
        rows, operands = chunk(n)
        order = plan[n][1]
        following = order[1] - (order[1] > order[0])
        *more, keeps[n], send = near(
            line, rows, order[0], following, operands, cames[n], shrunk if n == ride else None
        )
        shrunk = more[0] if more else shrunk
        cames[n] = swap(send, "tp", 2 << order[1], size)

    def end(n):
        nonlocal shrunk
        order = plan[n][1]
        for i in range(2, len(order)):
            left = order[i] - sum(order[i] > t for t in order[:i])
            *more, keeps[n], send = add(line, left, keeps[n], cames[n], shrunk if n == ride else None)
            shrunk = more[0] if more else shrunk
            cames[n] = swap(send, "tp", 2 << order[i], size)
        sums[n] = [keeps[n], cames[n]]

    cut_keep, cut_send = cut(line, shrink_panels, expand_panels, size, replicas)
    cut_came = swap(cut_send, "tp", 2, size)
    pieces = [spans[first_piece - 1].stop]
    if first_piece < len(plan):
        pieces.append(rows - pieces[0])
    attended, weight_own, picked, *attended_pieces = attend(
        line, queries, key_cache, value_cache, new_keys, new_values, cache_lengths, adapter_ids, out_weight, size, pieces
    )
    weight_other = swap(picked, "tp", 1, size)
    attended_other = [swap(piece, "tp", 1, size) for piece in attended_pieces]
    attended_all = [attended] + [swap(attended, "rep", k, replicas) for k in range(1, replicas)]

    shrunk = sent = panels = ranks = lora = None
    expanding_all = []
    for step in steps_list:
        name, n = (step[:-1], int(step[-1])) if step[-1].isdigit() else (step, 0)
        if name == "side":
            side_keep, *side_send = side(line, cut_keep, cut_came, ())
        elif name == "far":
            begin(n)
        elif name == "sort":
            panels = far_blocks(sort(line, side_keep, [swap(part, "tp", 1, size) for part in side_send]))
        elif name == "shrink":
            shrunk, sent = shrink(line, steps, panels, attended_all)
        elif name == "core":
            shrunk, sent = total(line, shrunk, swap(sent, "tp", 1, size))
        elif name == "ranks":
            rows_there = spans[ride].stop - spans[ride].start
            ranks = arrive(line, rows_there, shrunk, cames[ride])
            ranks = [ranks[0]] + [swap(ranks[k], "rep", k, replicas) for k in range(1, replicas)]
        elif name == "near":
            middle(n)
        elif name == "end":
            end(n)
        elif name == "fold":
            sums[n] = [fold(line, sums[n])]
        elif name == "expanding":
            expanding_all = [expanding(line, panels)]
            expanding_all += [swap(expanding_all[0], "rep", k, replicas) for k in range(1, replicas)]
        elif name == "expand":
            lora = expand(line, steps, adapter_ids, ranks, expanding_all)
        elif name == "have_x":
            line += attended_all[1:]
        elif name == "have_e":
            line += expanding_all[1:]
        elif name == "have":
            line.append(cames[n])
    order = sorted(range(last + 1), key=lambda n: len(sums[n]))
    ready = [sums[n][0] for n in order if len(sums[n]) == 1]
    terms = [x for n in order if len(sums[n]) == 2 for x in sums[n]]
    return finish([spans[n] for n in order], lora, ready, terms).reshape(queries.shape)


def solution(mesh):
    return jax.shard_map(
        functools.partial(body, mesh.shape["tp"], mesh.shape["rep"]),
        mesh=mesh,
        in_specs=(
            P(None, "rep", "tp"),
            P("rep", None, None),
            P("rep", None, None),
            P(None, "rep", None),
            P(None, "rep", None),
            P("rep"),
            P("rep", None),
            P("tp", None),
            P("tp", None, None),
            P("tp", None, None),
        ),
        out_specs=P(None, "rep", "tp"),
        check_vma=False,
    )
```

```python
import functools

import jax
import jax.numpy as jnp
from jax import lax
from jax.experimental import pallas as pl
from jax.experimental.pallas import tpu as pltpu
from jax.sharding import PartitionSpec as P

HD = 128
LANES = 128
GROUP_REQ = 16
VMEM_LIMIT = 24 << 20
F32 = jnp.float32
BF16 = jnp.bfloat16
PLAN = ((8, (0, 1, 2)), (4, (0, 1, 2)), (1, (0, 1, 2)), (3, (1, 0, 2)))
FIRST_PIECE = 4
RIDE = 2
STEPS = (
    "side",
    "far3",
    "far0",
    "sort",
    "have_x",
    "far1",
    "have3",
    "near0",
    "shrink",
    "core",
    "cross",
    "expanding",
    "far2",
    "near3",
    "near1",
    "end0",
    "near2",
    "end1",
    "fold0",
    "end3",
    "end2",
    "fold1",
    "ranks",
    "expand",
    "fold3",
)
PLAIN_STEPS = ("side", "sort", "shrink", "core", "cross", "far0", "near0", "end0", "ranks", "expanding", "expand")


def call(line, kernel, name, vmem, hbm, out, cost, scratch=(), after=()):
    operands = [pltpu.with_memory_space_constraint(x, pltpu.VMEM) for x in vmem]
    operands += [pltpu.with_memory_space_constraint(x, pltpu.HBM) for x in hbm]
    before = [*line, *after]
    count, extra = len(operands), len(before)

    def run(*refs):
        kernel(*refs[:count], *refs[count + extra :])

    results = pl.pallas_call(
        run,
        in_specs=[pl.BlockSpec(memory_space=pltpu.VMEM)] * len(vmem)
        + [pl.BlockSpec(memory_space=pltpu.HBM)] * len(hbm)
        + [pl.BlockSpec(memory_space=pl.ANY)] * extra,
        out_specs=[pl.BlockSpec(memory_space=pltpu.VMEM)] * len(out),
        out_shape=[pltpu.VMEM(shape, dtype) for shape, dtype in out],
        scratch_shapes=scratch,
        compiler_params=pltpu.CompilerParams(vmem_limit_bytes=VMEM_LIMIT),
        cost_estimate=pl.CostEstimate(flops=cost, bytes_accessed=1 << 16, transcendentals=0),
        name=name,
    )(*operands, *before)
    line[:] = [min(results, key=lambda x: x.size)]
    return results


def put_bit(i, position, value):
    low = i & ((1 << position) - 1)
    return ((i >> position) << (position + 1)) | (value << position) | low


def cut_copies(panel_ref, keep_ref, send_ref, panel, place, replica):
    groups, share, width = keep_ref.shape[2:]
    rank = pl.multiple_of(replica * share, share)
    copies = []
    for low, cut_ref in enumerate((keep_ref, keep_ref, send_ref, send_ref)):
        for high in range(groups):
            column = pl.multiple_of((place ^ (4 * high + low)) * width, width)
            copies.append(
                (panel_ref.at[0, pl.ds(rank, share), pl.ds(column, width)], cut_ref.at[low % 2, panel, high])
            )
    return copies


def run_copies(copies, sems):
    copies = [pltpu.make_async_copy(a, b, sems.at[i]) for i, (a, b) in enumerate(copies)]
    for copy in copies:
        copy.start()
    for copy in copies:
        copy.wait()


def pick_kernel(w_ref, shrink_ref, expand_ref, pick_ref, keep_ref, send_ref, sems):
    place, replica = lax.axis_index("tp"), lax.axis_index("rep")
    pairs, _, width = pick_ref.shape
    copies = []
    for i in range(pairs):
        column = pl.multiple_of((2 * (i ^ (place // 2)) + 1 - place % 2) * width, width)
        copies.append((w_ref.at[:, pl.ds(column, width)], pick_ref.at[i]))
    copies += cut_copies(shrink_ref, keep_ref, send_ref, 0, place, replica)
    copies += cut_copies(expand_ref, keep_ref, send_ref, 1, place, replica)
    run_copies(copies, sems)


def pick(line, weight, shrink_panels, expand_panels, size, replicas):
    depth, full = weight.shape
    pairs, width = size // 2, full // size
    cut = ((2, 2, size // 4, shrink_panels.shape[1] // replicas, width), BF16)
    return call(
        line,
        pick_kernel,
        "pick",
        (),
        (weight, shrink_panels, expand_panels),
        [((pairs, depth, width), BF16), cut, cut],
        0,
        scratch=[pltpu.SemaphoreType.DMA((pairs + 2 * size,))],
    )


def attention_kernel(
    lengths_ref, ids_ref, q_hbm, kc_hbm, vc_hbm, nk_hbm, nv_hbm, w_hbm, out_ref, own_ref, *rest
):
    *piece_refs, q_ref, kc_ref, vc_ref, nk_ref, nv_ref, q_sems, w_sems = rest
    place = lax.axis_index("tp")
    steps, requests, width = q_ref.shape
    heads = width // HD
    cached, fresh = kc_ref.shape[0], nk_ref.shape[0]
    block = own_ref.shape[2]
    size = 2 * own_ref.shape[0]
    group_heads = size * width // kc_hbm.shape[2]
    head = pl.multiple_of(place * heads // group_heads * HD, HD)
    parts = 2
    part = requests // parts
    loads = []
    for n in range(parts):
        span = pl.ds(n * part, part)
        pieces = [(q_hbm.at[:, span, :], q_ref.at[:, span, :])]
        for a, b in ((kc_hbm, kc_ref), (nk_hbm, nk_ref), (vc_hbm, vc_ref), (nv_hbm, nv_ref)):
            pieces.append((a.at[:, span, pl.ds(head, HD)], b.at[:, span, :]))
        loads.append([pltpu.make_async_copy(a, b, q_sems.at[n, i]) for i, (a, b) in enumerate(pieces)])
    pair, mine = place // 2, place % 2
    others = []
    for i in range(own_ref.shape[0]):
        column = pl.multiple_of((2 * (i ^ pair) + mine) * block, block)
        others.append((w_hbm.at[:, pl.ds(column, block)], own_ref.at[i]))
    others = [pltpu.make_async_copy(a, b, w_sems.at[i]) for i, (a, b) in enumerate(others)]
    for copy in [c for load in loads for c in load] + others:
        copy.start()

    group = GROUP_REQ
    rows, columns = steps * heads * group, (cached + fresh) * group
    row = lax.broadcasted_iota(jnp.int32, (rows, columns), 0)
    column = lax.broadcasted_iota(jnp.int32, (rows, columns), 1)
    same = row % group == column % group
    position = column // group
    step = row // (heads * group)
    fresh_ok = jnp.logical_and(position >= cached, position - cached <= step)
    column_position = lax.broadcasted_iota(jnp.int32, (1, columns), 1) // group
    tail = lax.broadcasted_iota(jnp.int32, (group, requests), 0) == 0
    out_ref[steps * requests :, :] = jnp.zeros((group, width), BF16)
    out_ref[steps * requests :, :requests] = jnp.where(tail, ids_ref[...].astype(F32), 0.0).astype(BF16)
    for n in range(parts):
        for copy in loads[n]:
            copy.wait()
        for i in range(n * part // group, (n + 1) * part // group):
            span = slice(i * group, (i + 1) * group)
            query = jnp.concatenate(
                [q_ref[s, span, h * HD : (h + 1) * HD] for s in range(steps) for h in range(heads)], 0
            )
            keys = jnp.concatenate(
                [kc_ref[p, span, :] for p in range(cached)] + [nk_ref[s, span, :] for s in range(fresh)], 0
            )
            values = jnp.concatenate(
                [vc_ref[p, span, :] for p in range(cached)] + [nv_ref[s, span, :] for s in range(fresh)], 0
            )
            scores = lax.dot_general(
                query, keys, (((1,), (1,)), ((), ())), preferred_element_type=F32
            ) * (1.0 / HD**0.5)
            limit = jnp.concatenate([lengths_ref[:, span]] * (cached + fresh), 1)
            cached_ok = column_position < limit
            visible = jnp.logical_and(same, jnp.logical_or(cached_ok, fresh_ok))
            scores = jnp.where(visible, scores, -1e30)
            scaled = jnp.exp(scores - scores.max(-1, keepdims=True))
            weights = (scaled / scaled.sum(-1, keepdims=True)).astype(BF16)
            mixed = jnp.dot(weights, values, preferred_element_type=F32).astype(BF16)
            for s in range(steps):
                for h in range(heads):
                    at = (s * heads + h) * group
                    to = s * requests + i * group
                    out_ref[to : to + group, h * HD : (h + 1) * HD] = mixed[at : at + group, :]
    first = 0
    for piece_ref in piece_refs:
        piece_ref[...] = out_ref[first : first + piece_ref.shape[0], :]
        first += piece_ref.shape[0]
    for copy in others:
        copy.wait()


def attend(line, queries, key_cache, value_cache, new_keys, new_values, cache_lengths, adapter_ids, weight, size, pieces):
    steps, requests, width = queries.shape
    cached = key_cache.shape[1]
    depth, full = weight.shape
    block, pairs = full // size, size // 2
    return call(
        line,
        attention_kernel,
        "attention",
        (cache_lengths.reshape(1, -1), adapter_ids.reshape(1, -1)),
        (queries, key_cache.transpose(1, 0, 2), value_cache.transpose(1, 0, 2), new_keys, new_values, weight),
        [
            ((steps * requests + GROUP_REQ, width), BF16),
            ((pairs, depth, block), BF16),
        ]
        + [((piece, width), BF16) for piece in pieces],
        4 * requests * steps * width * (cached + steps) * GROUP_REQ,
        [
            pltpu.VMEM((steps, requests, width), BF16),
            pltpu.VMEM((cached, requests, HD), BF16),
            pltpu.VMEM((cached, requests, HD), BF16),
            pltpu.VMEM((steps, requests, HD), BF16),
            pltpu.VMEM((steps, requests, HD), BF16),
            pltpu.SemaphoreType.DMA((2, 5)),
            pltpu.SemaphoreType.DMA((pairs,)),
        ],
    )


def product(spans, which, a_ref, b_ref, own_ref, other_ref):
    return jnp.dot(a_ref[spans[0], :], own_ref[which], preferred_element_type=F32) + jnp.dot(
        b_ref[spans[1], :], other_ref[which], preferred_element_type=F32
    )


def pack(small, blocks, width):
    part = small.shape[0] // blocks
    fold = part * LANES // width
    return [
        jnp.concatenate([small[i * part + j : i * part + j + fold] for j in range(0, part, fold)], 1)
        for i in range(blocks)
    ]


def unpack(blocks):
    return jnp.concatenate(
        [block[:, j : j + LANES] for block in blocks for j in range(0, block.shape[1], LANES)], 0
    )


def extra_rows(small, blocks, width):
    return 0 if small is None else small.size // (blocks * width)


def pass_small(small_ref, arrived_ref, more_ref, send_ref, rows):
    flat = small_ref[...].reshape(-1, LANES)
    flat = flat + unpack([arrived_ref[i, rows:, :].astype(F32) for i in range(arrived_ref.shape[0])])
    more_ref[...] = flat.reshape(more_ref.shape)
    if send_ref is not None:
        for i, block in enumerate(pack(flat.astype(BF16), send_ref.shape[0], send_ref.shape[2])):
            send_ref[i, rows:, :] = block


def far_kernel(spans, stage, *refs):
    operands, sent_refs, out_ref = refs[:4], refs[4:-1], refs[-1]
    rows = spans[0].stop - spans[0].start
    for i in range(out_ref.shape[0]):
        out_ref[i, :rows, :] = product(spans, put_bit(i, stage, 1), *operands).astype(BF16)
    for sent_ref in sent_refs:
        for i, block in enumerate(pack(sent_ref[...].reshape(-1, LANES), out_ref.shape[0], out_ref.shape[2])):
            out_ref[i, rows:, :] = block


def far(line, spans, stage, operands, sent=None):
    pairs, depth, width = operands[2].shape
    rows = spans[0].stop - spans[0].start
    more = extra_rows(sent, pairs // 2, width)
    return call(
        line,
        functools.partial(far_kernel, spans, stage),
        "far",
        operands if sent is None else (*operands, sent),
        (),
        [((pairs // 2, rows + more, width), BF16)],
        2 * rows * depth * pairs * width,
    )[0]


def near_kernel(spans, stage, following, *refs):
    operands, arrived_ref, refs = refs[:4], refs[4], refs[5:]
    rows = spans[0].stop - spans[0].start
    keep_ref, send_ref = refs[-2:]
    for i in range(keep_ref.shape[0]):
        for value, out_ref in ((1, send_ref), (0, keep_ref)):
            at = put_bit(i, following, value)
            total = product(spans, put_bit(at, stage, 0), *operands) + arrived_ref[at, :rows, :].astype(F32)
            out_ref[i, :rows, :] = total.astype(out_ref.dtype)
    if len(refs) > 2:
        pass_small(refs[0], arrived_ref, refs[1], send_ref, rows)


def near(line, spans, stage, following, operands, arrived, small=None):
    pairs, depth, width = operands[2].shape
    rows = spans[0].stop - spans[0].start
    more = extra_rows(small, pairs // 4, width)
    return call(
        line,
        functools.partial(near_kernel, spans, stage, following),
        "near",
        (*operands, arrived) if small is None else (*operands, arrived, small),
        (),
        ([] if small is None else [(small.shape, F32)])
        + [((pairs // 4, rows, width), F32), ((pairs // 4, rows + more, width), BF16)],
        2 * rows * depth * pairs * width,
    )


def add_kernel(following, keep_ref, arrived_ref, *refs):
    more_ref, send_ref = refs[-2:]
    rows = keep_ref.shape[1]
    for i in range(more_ref.shape[0]):
        for value, out_ref in ((1, send_ref), (0, more_ref)):
            at = put_bit(i, following, value)
            total = keep_ref[at] + arrived_ref[at, :rows, :].astype(F32)
            out_ref[i, :rows, :] = total.astype(out_ref.dtype)
    if len(refs) > 2:
        pass_small(refs[0], arrived_ref, refs[1], send_ref, rows)


def add(line, following, keep, arrived, small=None):
    blocks, rows, width = keep.shape
    more = extra_rows(small, blocks // 2, width)
    return call(
        line,
        functools.partial(add_kernel, following),
        "add",
        (keep, arrived) if small is None else (keep, arrived, small),
        (),
        ([] if small is None else [(small.shape, F32)])
        + [((blocks // 2, rows, width), F32), ((blocks // 2, rows + more, width), BF16)],
        2 * keep.size,
    )


def total_kernel(a_ref, b_ref, out_ref, *sent_refs):
    out_ref[...] = a_ref[...] + b_ref[...].astype(F32)
    for k, sent_ref in enumerate(sent_refs):
        sent_ref[...] = out_ref[k + 1].astype(BF16)


def total(line, a, b):
    out = [(a.shape, F32)] + [(a.shape[1:], BF16)] * (a.shape[0] - 1)
    return call(line, total_kernel, "total", (a, b), (), out, a.size)


def cross_kernel(a_ref, *refs):
    arrived_refs, (out_ref, sent_ref) = refs[:-2], refs[-2:]
    out_ref[0] = a_ref[0]
    for k, ref in enumerate(arrived_refs):
        out_ref[k + 1] = ref[...].astype(F32)
    sent_ref[...] = out_ref[...].astype(BF16)


def cross(line, a, arrived):
    return call(line, cross_kernel, "cross", (a, *arrived), (), [(a.shape, F32), (a.shape, BF16)], 0)


def arrive_kernel(rows, small_ref, arrived_ref, *out_refs):
    flat = small_ref[...].reshape(-1, LANES) + unpack([arrived_ref[0, rows:, :].astype(F32)])
    small = flat.reshape(small_ref.shape).astype(BF16)
    for k, out_ref in enumerate(out_refs):
        out_ref[...] = small[k]


def arrive(line, rows, small, arrived):
    out = [(small.shape[1:], BF16)] * small.shape[0]
    return call(line, functools.partial(arrive_kernel, rows), "arrive", (small, arrived), (), out, 0)


def side_kernel(keep_ref, arrived_ref, more_ref, *send_refs):
    for source, ref in enumerate((keep_ref, arrived_ref)):
        more_ref[source] = ref[0]
        for panel, send_ref in enumerate(send_refs):
            send_ref[source] = ref[1, panel]


def side(line, keep, arrived, after):
    part = (keep.shape[:1] + keep.shape[2:], BF16)
    return call(line, side_kernel, "side", (keep, arrived), (), [(keep.shape, BF16), part, part], 0, after=after)


def sort_kernel(keep_ref, *refs):
    arrived_refs, out_refs = refs[:2], refs[2:]
    for high, out_ref in enumerate(out_refs):
        for side in range(2):
            for panel in range(2):
                out_ref[panel, 2 * side] = keep_ref[side, panel, high]
                out_ref[panel, 2 * side + 1] = arrived_refs[panel][side, high]


def sort(line, keep, arrived):
    groups, share, width = keep.shape[2:]
    return call(line, sort_kernel, "sort", (keep, *arrived), (), [((2, 4, share, width), BF16)] * groups, 0)


def far_blocks(blocks):
    size = 4 * len(blocks)
    return [blocks[0]] + [swap(b, "tp", 4 * h, size) for h, b in enumerate(blocks) if h]


def expanding_kernel(*refs):
    out_ref = refs[-1]
    for high, ref in enumerate(refs[:-1]):
        for source in range(4):
            out_ref[4 * high + source] = ref[1, source]


def expanding(line, blocks):
    share, width = blocks[0].shape[2:]
    out = [((4 * len(blocks), share, width), BF16)]
    return call(line, expanding_kernel, "expanding", blocks, (), out, 0)[0]


def owners(ids, shape, high, share):
    owner = 4 * high + lax.broadcasted_iota(jnp.int32, shape, 1) // share
    return owner == (ids ^ lax.axis_index("tp"))


def shrink_kernel(steps, groups, *refs):
    panels, attended, out_refs = refs[:groups], refs[groups:-2], refs[-2:]
    share, width = panels[0].shape[2:]
    for k, a_ref in enumerate(attended):
        rows = a_ref.shape[0] - GROUP_REQ
        requests = rows // steps
        row = lax.broadcasted_iota(jnp.int32, (requests, requests), 0)
        column = lax.broadcasted_iota(jnp.int32, (requests, requests), 1)
        line = a_ref[rows : rows + GROUP_REQ, :requests].astype(F32)[:1, :]
        ids = jnp.where(row == column, line, 0.0).sum(1, keepdims=True).astype(jnp.int32)
        ids = jnp.concatenate([ids] * steps, 0)
        total = None
        for high, panel in enumerate(panels):
            flat = panel[0].reshape(4 * share, width)
            ranks = lax.dot_general(
                a_ref[:rows, :], flat, (((1,), (1,)), ((), ())), preferred_element_type=F32
            )
            ranks = jnp.where(owners(ids, ranks.shape, high, share), ranks, 0.0)
            total = ranks if total is None else total + ranks
        part = total[:, :share]
        for i in range(1, 4):
            part = part + total[:, share * i : share * (i + 1)]
        fold = out_refs[0].shape[1]
        part = jnp.concatenate([part[i * fold : (i + 1) * fold] for i in range(rows // fold)], 1)
        for out_ref in out_refs:
            out_ref[k] = part.astype(out_ref.dtype)


def shrink(line, steps, panels, attended):
    replicas, rows, share = len(attended), attended[0].shape[0] - GROUP_REQ, panels[0].shape[2]
    return call(
        line,
        functools.partial(shrink_kernel, steps, len(panels)),
        "shrink",
        (*panels, *attended),
        (),
        [((replicas, rows * share // LANES, LANES), dtype) for dtype in (F32, BF16)],
        2 * rows * replicas * len(panels) * panels[0].size,
    )


def expand_kernel(steps, replicas, ids_ref, *refs):
    ranks, panels, out_ref = refs[:replicas], refs[replicas:-1], refs[-1]
    _, share, width = panels[0].shape
    ids = jnp.concatenate([ids_ref[...]] * steps, 0)
    total = None
    for k, rank_ref in enumerate(ranks):
        folded = rank_ref[...].astype(F32)
        part = jnp.concatenate([folded[:, i * share : (i + 1) * share] for i in range(LANES // share)], 0)
        part = jnp.concatenate([part] * 4, 1)
        panel = panels[k]
        spread = [
            jnp.where(owners(ids, part.shape, high, share), part, 0.0).astype(BF16)
            for high in range(panel.shape[0] // 4)
        ]
        term = jnp.dot(
            jnp.concatenate(spread, 1), panel[...].reshape(-1, width), preferred_element_type=F32
        )
        total = term if total is None else total + term
    out_ref[...] = total


def expand(line, steps, ids, ranks, panels):
    rows, width = steps * ids.shape[0], panels[0].shape[2]
    return call(
        line,
        functools.partial(expand_kernel, steps, len(ranks)),
        "expand",
        (ids, *ranks, *panels),
        (),
        [((rows, width), F32)],
        2 * rows * len(panels) * panels[0].size,
    )[0]


def fold_kernel(keep_ref, arrived_ref, out_ref):
    out_ref[...] = keep_ref[0] + arrived_ref[0, : keep_ref.shape[1], :].astype(F32)


def fold(line, terms):
    return call(line, fold_kernel, "fold", terms, (), [(terms[0].shape[1:], F32)], 0)[0]


def finish_kernel(spans, folded, lora_ref, *refs):
    refs, out_ref = refs[:-1], refs[-1]
    for n, span in enumerate(spans):
        if n < folded:
            total = refs[n][...]
        else:
            keep_ref, arrived_ref = refs[2 * n - folded : 2 * n - folded + 2]
            total = keep_ref[0] + arrived_ref[0, : keep_ref.shape[1], :].astype(F32)
        out_ref[span, :] = (total + lora_ref[span, :]).astype(BF16)


def finish(spans, lora, sums, terms):
    operands = [pltpu.with_memory_space_constraint(x, pltpu.VMEM) for x in (lora, *sums, *terms)]
    return pl.pallas_call(
        functools.partial(finish_kernel, spans, len(sums)),
        in_specs=[pl.BlockSpec(memory_space=pltpu.VMEM)] * len(operands),
        out_specs=pl.BlockSpec(memory_space=pltpu.VMEM),
        out_shape=jax.ShapeDtypeStruct(lora.shape, BF16),
        compiler_params=pltpu.CompilerParams(vmem_limit_bytes=VMEM_LIMIT),
        cost_estimate=pl.CostEstimate(flops=4 * lora.size, bytes_accessed=1 << 20, transcendentals=0),
        name="finish",
    )(*operands)


def swap(array, axis, bit, size):
    return lax.ppermute(array, axis, [(i, i ^ bit) for i in range(size)])


def body(
    size,
    replicas,
    queries,
    key_cache,
    value_cache,
    new_keys,
    new_values,
    cache_lengths,
    adapter_ids,
    out_weight,
    shrink_panels,
    expand_panels,
):
    steps, requests, local = queries.shape
    rows = steps * requests
    pairs = size // 2
    stages = size.bit_length() - 2
    if stages == 3:
        plan, first_piece, ride, steps_list = PLAN, FIRST_PIECE, RIDE, STEPS
    else:
        plan, first_piece, ride, steps_list = ((16, tuple(range(stages))),), 1, 0, PLAIN_STEPS
    spans, first = [], 0
    for part, _ in plan:
        spans.append(slice(first, first + rows * part // 16))
        first += rows * part // 16

    line = []
    last = len(plan) - 1
    keeps, cames, sums = {}, {}, {}

    def chunk(n):
        piece = 0 if n < first_piece else 1
        start = spans[first_piece].start if piece else 0
        there = slice(spans[n].start - start, spans[n].stop - start)
        return (spans[n], there), (attended, attended_other[piece], weight_own, weight_other)

    def begin(n):
        rows, operands = chunk(n)
        order = plan[n][1]
        block = far(line, rows, order[0], operands, sent if n == ride else None)
        cames[n] = swap(block, "tp", 2 << order[0], size)

    def middle(n):
        nonlocal shrunk
        rows, operands = chunk(n)
        order = plan[n][1]
        following = order[1] - (order[1] > order[0])
        *more, keeps[n], send = near(
            line, rows, order[0], following, operands, cames[n], shrunk if n == ride else None
        )
        shrunk = more[0] if more else shrunk
        cames[n] = swap(send, "tp", 2 << order[1], size)

    def end(n):
        nonlocal shrunk
        order = plan[n][1]
        for i in range(2, len(order)):
            left = order[i] - sum(order[i] > t for t in order[:i])
            *more, keeps[n], send = add(line, left, keeps[n], cames[n], shrunk if n == ride else None)
            shrunk = more[0] if more else shrunk
            cames[n] = swap(send, "tp", 2 << order[i], size)
        sums[n] = [keeps[n], cames[n]]

    picked, cut_keep, cut_send = pick(line, out_weight, shrink_panels, expand_panels, size, replicas)
    weight_other = swap(picked, "tp", 1, size)
    cut_came = swap(cut_send, "tp", 2, size)
    pieces = [spans[first_piece - 1].stop]
    if first_piece < len(plan):
        pieces.append(rows - pieces[0])
    attended, weight_own, *attended_pieces = attend(
        line, queries, key_cache, value_cache, new_keys, new_values, cache_lengths, adapter_ids, out_weight, size, pieces
    )
    attended_other = [swap(piece, "tp", 1, size) for piece in attended_pieces]
    attended_all = [attended] + [swap(attended, "rep", k, replicas) for k in range(1, replicas)]

    shrunk = sent = panels = ranks = lora = None
    expanding_all = []
    for step in steps_list:
        name, n = (step[:-1], int(step[-1])) if step[-1].isdigit() else (step, 0)
        if name == "side":
            side_keep, *side_send = side(line, cut_keep, cut_came, ())
        elif name == "far":
            begin(n)
        elif name == "sort":
            panels = far_blocks(sort(line, side_keep, [swap(part, "tp", 1, size) for part in side_send]))
        elif name == "shrink":
            shrunk, sent = shrink(line, steps, panels, attended_all)
        elif name == "core":
            shrunk, *parts = total(line, shrunk, swap(sent, "tp", 1, size))
            parts = [swap(part, "rep", k + 1, replicas) for k, part in enumerate(parts)]
        elif name == "cross":
            shrunk, sent = cross(line, shrunk, parts)
        elif name == "ranks":
            rows_there = spans[ride].stop - spans[ride].start
            ranks = arrive(line, rows_there, shrunk, cames[ride])
        elif name == "near":
            middle(n)
        elif name == "end":
            end(n)
        elif name == "fold":
            sums[n] = [fold(line, sums[n])]
        elif name == "expanding":
            expanding_all = [expanding(line, panels)]
            expanding_all += [swap(expanding_all[0], "rep", k, replicas) for k in range(1, replicas)]
        elif name == "expand":
            lora = expand(line, steps, adapter_ids, ranks, expanding_all)
        elif name == "have_x":
            line += attended_all[1:]
        elif name == "have_e":
            line += expanding_all[1:]
        elif name == "have":
            line.append(cames[n])
    order = sorted(range(last + 1), key=lambda n: len(sums[n]))
    ready = [sums[n][0] for n in order if len(sums[n]) == 1]
    terms = [x for n in order if len(sums[n]) == 2 for x in sums[n]]
    return finish([spans[n] for n in order], lora, ready, terms).reshape(queries.shape)


def solution(mesh):
    return jax.shard_map(
        functools.partial(body, mesh.shape["tp"], mesh.shape["rep"]),
        mesh=mesh,
        in_specs=(
            P(None, "rep", "tp"),
            P("rep", None, None),
            P("rep", None, None),
            P(None, "rep", None),
            P(None, "rep", None),
            P("rep"),
            P("rep", None),
            P("tp", None),
            P("tp", None, None),
            P("tp", None, None),
        ),
        out_specs=P(None, "rep", "tp"),
        check_vma=False,
    )
```

```python
import functools

import jax
import jax.numpy as jnp
from jax import lax
from jax.experimental import pallas as pl
from jax.experimental.pallas import tpu as pltpu
from jax.sharding import PartitionSpec as P

HD = 128
LANES = 128
GROUP_REQ = 16
VMEM_LIMIT = 24 << 20
F32 = jnp.float32
BF16 = jnp.bfloat16
PLAN = ((8, (0, 1, 2)), (4, (0, 1, 2)), (1, (0, 1, 2)), (3, (1, 0, 2)))
FIRST_PIECE = 4
RIDE = 2
STEPS = (
    "side",
    "far3",
    "far0",
    "sort",
    "have_x",
    "far1",
    "have3",
    "near0",
    "shrink",
    "core",
    "cross",
    "expanding",
    "far2",
    "near1",
    "end0",
    "near3",
    "near2",
    "end1",
    "fold0",
    "end3",
    "end2",
    "fold1",
    "ranks",
    "expand",
    "fold3",
)
PLAIN_STEPS = ("side", "sort", "shrink", "core", "cross", "far0", "near0", "end0", "ranks", "expanding", "expand")


def call(line, kernel, name, vmem, hbm, out, cost, scratch=(), after=()):
    operands = [pltpu.with_memory_space_constraint(x, pltpu.VMEM) for x in vmem]
    operands += [pltpu.with_memory_space_constraint(x, pltpu.HBM) for x in hbm]
    before = [*line, *after]
    count, extra = len(operands), len(before)

    def run(*refs):
        kernel(*refs[:count], *refs[count + extra :])

    results = pl.pallas_call(
        run,
        in_specs=[pl.BlockSpec(memory_space=pltpu.VMEM)] * len(vmem)
        + [pl.BlockSpec(memory_space=pltpu.HBM)] * len(hbm)
        + [pl.BlockSpec(memory_space=pl.ANY)] * extra,
        out_specs=[pl.BlockSpec(memory_space=pltpu.VMEM)] * len(out),
        out_shape=[pltpu.VMEM(shape, dtype) for shape, dtype in out],
        scratch_shapes=scratch,
        compiler_params=pltpu.CompilerParams(vmem_limit_bytes=VMEM_LIMIT),
        cost_estimate=pl.CostEstimate(flops=cost, bytes_accessed=1 << 16, transcendentals=0),
        name=name,
    )(*operands, *before)
    line[:] = [min(results, key=lambda x: x.size)]
    return results


def put_bit(i, position, value):
    low = i & ((1 << position) - 1)
    return ((i >> position) << (position + 1)) | (value << position) | low


def cut_copies(panel_ref, keep_ref, send_ref, panel, place, replica):
    groups, share, width = keep_ref.shape[2:]
    rank = pl.multiple_of(replica * share, share)
    copies = []
    for low, cut_ref in enumerate((keep_ref, keep_ref, send_ref, send_ref)):
        for high in range(groups):
            column = pl.multiple_of((place ^ (4 * high + low)) * width, width)
            copies.append(
                (panel_ref.at[0, pl.ds(rank, share), pl.ds(column, width)], cut_ref.at[low % 2, panel, high])
            )
    return copies


def run_copies(copies, sems):
    copies = [pltpu.make_async_copy(a, b, sems.at[i]) for i, (a, b) in enumerate(copies)]
    for copy in copies:
        copy.start()
    for copy in copies:
        copy.wait()


def pick_kernel(w_ref, shrink_ref, expand_ref, pick_ref, keep_ref, send_ref, sems):
    place, replica = lax.axis_index("tp"), lax.axis_index("rep")
    pairs, _, width = pick_ref.shape
    copies = []
    for i in range(pairs):
        column = pl.multiple_of((2 * (i ^ (place // 2)) + 1 - place % 2) * width, width)
        copies.append((w_ref.at[:, pl.ds(column, width)], pick_ref.at[i]))
    copies += cut_copies(shrink_ref, keep_ref, send_ref, 0, place, replica)
    copies += cut_copies(expand_ref, keep_ref, send_ref, 1, place, replica)
    run_copies(copies, sems)


def pick(line, weight, shrink_panels, expand_panels, size, replicas):
    depth, full = weight.shape
    pairs, width = size // 2, full // size
    cut = ((2, 2, size // 4, shrink_panels.shape[1] // replicas, width), BF16)
    return call(
        line,
        pick_kernel,
        "pick",
        (),
        (weight, shrink_panels, expand_panels),
        [((pairs, depth, width), BF16), cut, cut],
        0,
        scratch=[pltpu.SemaphoreType.DMA((pairs + 2 * size,))],
    )


def attention_kernel(
    lengths_ref, ids_ref, q_hbm, kc_hbm, vc_hbm, nk_hbm, nv_hbm, w_hbm, out_ref, own_ref, *rest
):
    *piece_refs, q_ref, kc_ref, vc_ref, nk_ref, nv_ref, q_sems, w_sems = rest
    place = lax.axis_index("tp")
    steps, requests, width = q_ref.shape
    heads = width // HD
    cached, fresh = kc_ref.shape[0], nk_ref.shape[0]
    block = own_ref.shape[2]
    size = 2 * own_ref.shape[0]
    group_heads = size * width // kc_hbm.shape[2]
    head = pl.multiple_of(place * heads // group_heads * HD, HD)
    parts = 2
    part = requests // parts
    loads = []
    for n in range(parts):
        span = pl.ds(n * part, part)
        pieces = [(q_hbm.at[:, span, :], q_ref.at[:, span, :])]
        for a, b in ((kc_hbm, kc_ref), (nk_hbm, nk_ref), (vc_hbm, vc_ref), (nv_hbm, nv_ref)):
            pieces.append((a.at[:, span, pl.ds(head, HD)], b.at[:, span, :]))
        loads.append([pltpu.make_async_copy(a, b, q_sems.at[n, i]) for i, (a, b) in enumerate(pieces)])
    pair, mine = place // 2, place % 2
    others = []
    for i in range(own_ref.shape[0]):
        column = pl.multiple_of((2 * (i ^ pair) + mine) * block, block)
        others.append((w_hbm.at[:, pl.ds(column, block)], own_ref.at[i]))
    others = [pltpu.make_async_copy(a, b, w_sems.at[i]) for i, (a, b) in enumerate(others)]
    for copy in [c for load in loads for c in load] + others:
        copy.start()

    group = GROUP_REQ
    rows, columns = steps * heads * group, (cached + fresh) * group
    row = lax.broadcasted_iota(jnp.int32, (rows, columns), 0)
    column = lax.broadcasted_iota(jnp.int32, (rows, columns), 1)
    same = row % group == column % group
    position = column // group
    step = row // (heads * group)
    fresh_ok = jnp.logical_and(position >= cached, position - cached <= step)
    column_position = lax.broadcasted_iota(jnp.int32, (1, columns), 1) // group
    tail = lax.broadcasted_iota(jnp.int32, (group, requests), 0) == 0
    out_ref[steps * requests :, :] = jnp.zeros((group, width), BF16)
    out_ref[steps * requests :, :requests] = jnp.where(tail, ids_ref[...].astype(F32), 0.0).astype(BF16)
    for n in range(parts):
        for copy in loads[n]:
            copy.wait()
        for i in range(n * part // group, (n + 1) * part // group):
            span = slice(i * group, (i + 1) * group)
            query = jnp.concatenate(
                [q_ref[s, span, h * HD : (h + 1) * HD] for s in range(steps) for h in range(heads)], 0
            )
            keys = jnp.concatenate(
                [kc_ref[p, span, :] for p in range(cached)] + [nk_ref[s, span, :] for s in range(fresh)], 0
            )
            values = jnp.concatenate(
                [vc_ref[p, span, :] for p in range(cached)] + [nv_ref[s, span, :] for s in range(fresh)], 0
            )
            scores = lax.dot_general(
                query, keys, (((1,), (1,)), ((), ())), preferred_element_type=F32
            ) * (1.0 / HD**0.5)
            limit = jnp.concatenate([lengths_ref[:, span]] * (cached + fresh), 1)
            cached_ok = column_position < limit
            visible = jnp.logical_and(same, jnp.logical_or(cached_ok, fresh_ok))
            scores = jnp.where(visible, scores, -1e30)
            scaled = jnp.exp(scores - scores.max(-1, keepdims=True))
            weights = (scaled / scaled.sum(-1, keepdims=True)).astype(BF16)
            mixed = jnp.dot(weights, values, preferred_element_type=F32).astype(BF16)
            for s in range(steps):
                for h in range(heads):
                    at = (s * heads + h) * group
                    to = s * requests + i * group
                    out_ref[to : to + group, h * HD : (h + 1) * HD] = mixed[at : at + group, :]
    first = 0
    for piece_ref in piece_refs:
        piece_ref[...] = out_ref[first : first + piece_ref.shape[0], :]
        first += piece_ref.shape[0]
    for copy in others:
        copy.wait()


def attend(line, queries, key_cache, value_cache, new_keys, new_values, cache_lengths, adapter_ids, weight, size, pieces):
    steps, requests, width = queries.shape
    cached = key_cache.shape[1]
    depth, full = weight.shape
    block, pairs = full // size, size // 2
    return call(
        line,
        attention_kernel,
        "attention",
        (cache_lengths.reshape(1, -1), adapter_ids.reshape(1, -1)),
        (queries, key_cache.transpose(1, 0, 2), value_cache.transpose(1, 0, 2), new_keys, new_values, weight),
        [
            ((steps * requests + GROUP_REQ, width), BF16),
            ((pairs, depth, block), BF16),
        ]
        + [((piece, width), BF16) for piece in pieces],
        4 * requests * steps * width * (cached + steps) * GROUP_REQ,
        [
            pltpu.VMEM((steps, requests, width), BF16),
            pltpu.VMEM((cached, requests, HD), BF16),
            pltpu.VMEM((cached, requests, HD), BF16),
            pltpu.VMEM((steps, requests, HD), BF16),
            pltpu.VMEM((steps, requests, HD), BF16),
            pltpu.SemaphoreType.DMA((2, 5)),
            pltpu.SemaphoreType.DMA((pairs,)),
        ],
    )


def product(spans, which, a_ref, b_ref, own_ref, other_ref):
    return jnp.dot(a_ref[spans[0], :], own_ref[which], preferred_element_type=F32) + jnp.dot(
        b_ref[spans[1], :], other_ref[which], preferred_element_type=F32
    )


def pack(small, blocks, width):
    part = small.shape[0] // blocks
    fold = part * LANES // width
    return [
        jnp.concatenate([small[i * part + j : i * part + j + fold] for j in range(0, part, fold)], 1)
        for i in range(blocks)
    ]


def unpack(blocks):
    return jnp.concatenate(
        [block[:, j : j + LANES] for block in blocks for j in range(0, block.shape[1], LANES)], 0
    )


def extra_rows(small, blocks, width):
    return 0 if small is None else small.size // (blocks * width)


def pass_small(small_ref, arrived_ref, more_ref, send_ref, rows):
    flat = small_ref[...].reshape(-1, LANES)
    flat = flat + unpack([arrived_ref[i, rows:, :].astype(F32) for i in range(arrived_ref.shape[0])])
    more_ref[...] = flat.reshape(more_ref.shape)
    if send_ref is not None:
        for i, block in enumerate(pack(flat.astype(BF16), send_ref.shape[0], send_ref.shape[2])):
            send_ref[i, rows:, :] = block


def far_kernel(spans, stage, *refs):
    operands, sent_refs, out_ref = refs[:4], refs[4:-1], refs[-1]
    rows = spans[0].stop - spans[0].start
    for i in range(out_ref.shape[0]):
        out_ref[i, :rows, :] = product(spans, put_bit(i, stage, 1), *operands).astype(BF16)
    for sent_ref in sent_refs:
        for i, block in enumerate(pack(sent_ref[...].reshape(-1, LANES), out_ref.shape[0], out_ref.shape[2])):
            out_ref[i, rows:, :] = block


def far(line, spans, stage, operands, sent=None):
    pairs, depth, width = operands[2].shape
    rows = spans[0].stop - spans[0].start
    more = extra_rows(sent, pairs // 2, width)
    return call(
        line,
        functools.partial(far_kernel, spans, stage),
        "far",
        operands if sent is None else (*operands, sent),
        (),
        [((pairs // 2, rows + more, width), BF16)],
        2 * rows * depth * pairs * width,
    )[0]


def near_kernel(spans, stage, following, *refs):
    operands, arrived_ref, refs = refs[:4], refs[4], refs[5:]
    rows = spans[0].stop - spans[0].start
    keep_ref, send_ref = refs[-2:]
    for i in range(keep_ref.shape[0]):
        for value, out_ref in ((1, send_ref), (0, keep_ref)):
            at = put_bit(i, following, value)
            total = product(spans, put_bit(at, stage, 0), *operands) + arrived_ref[at, :rows, :].astype(F32)
            out_ref[i, :rows, :] = total.astype(out_ref.dtype)
    if len(refs) > 2:
        pass_small(refs[0], arrived_ref, refs[1], send_ref, rows)


def near(line, spans, stage, following, operands, arrived, small=None):
    pairs, depth, width = operands[2].shape
    rows = spans[0].stop - spans[0].start
    more = extra_rows(small, pairs // 4, width)
    return call(
        line,
        functools.partial(near_kernel, spans, stage, following),
        "near",
        (*operands, arrived) if small is None else (*operands, arrived, small),
        (),
        ([] if small is None else [(small.shape, F32)])
        + [((pairs // 4, rows, width), F32), ((pairs // 4, rows + more, width), BF16)],
        2 * rows * depth * pairs * width,
    )


def add_kernel(following, keep_ref, arrived_ref, *refs):
    more_ref, send_ref = refs[-2:]
    rows = keep_ref.shape[1]
    for i in range(more_ref.shape[0]):
        for value, out_ref in ((1, send_ref), (0, more_ref)):
            at = put_bit(i, following, value)
            total = keep_ref[at] + arrived_ref[at, :rows, :].astype(F32)
            out_ref[i, :rows, :] = total.astype(out_ref.dtype)
    if len(refs) > 2:
        pass_small(refs[0], arrived_ref, refs[1], send_ref, rows)


def add(line, following, keep, arrived, small=None):
    blocks, rows, width = keep.shape
    more = extra_rows(small, blocks // 2, width)
    return call(
        line,
        functools.partial(add_kernel, following),
        "add",
        (keep, arrived) if small is None else (keep, arrived, small),
        (),
        ([] if small is None else [(small.shape, F32)])
        + [((blocks // 2, rows, width), F32), ((blocks // 2, rows + more, width), BF16)],
        2 * keep.size,
    )


def total_kernel(a_ref, b_ref, out_ref, *sent_refs):
    out_ref[...] = a_ref[...] + b_ref[...].astype(F32)
    for k, sent_ref in enumerate(sent_refs):
        sent_ref[...] = out_ref[k + 1].astype(BF16)


def total(line, a, b):
    out = [(a.shape, F32)] + [(a.shape[1:], BF16)] * (a.shape[0] - 1)
    return call(line, total_kernel, "total", (a, b), (), out, a.size)


def cross_kernel(a_ref, *refs):
    arrived_refs, (out_ref, sent_ref) = refs[:-2], refs[-2:]
    out_ref[0] = a_ref[0]
    for k, ref in enumerate(arrived_refs):
        out_ref[k + 1] = ref[...].astype(F32)
    sent_ref[...] = out_ref[...].astype(BF16)


def cross(line, a, arrived):
    return call(line, cross_kernel, "cross", (a, *arrived), (), [(a.shape, F32), (a.shape, BF16)], 0)


def arrive_kernel(rows, small_ref, arrived_ref, *out_refs):
    flat = small_ref[...].reshape(-1, LANES) + unpack([arrived_ref[0, rows:, :].astype(F32)])
    small = flat.reshape(small_ref.shape).astype(BF16)
    for k, out_ref in enumerate(out_refs):
        out_ref[...] = small[k]


def arrive(line, rows, small, arrived):
    out = [(small.shape[1:], BF16)] * small.shape[0]
    return call(line, functools.partial(arrive_kernel, rows), "arrive", (small, arrived), (), out, 0)


def side_kernel(keep_ref, arrived_ref, more_ref, *send_refs):
    for source, ref in enumerate((keep_ref, arrived_ref)):
        more_ref[source] = ref[0]
        for panel, send_ref in enumerate(send_refs):
            send_ref[source] = ref[1, panel]


def side(line, keep, arrived, after):
    part = (keep.shape[:1] + keep.shape[2:], BF16)
    return call(line, side_kernel, "side", (keep, arrived), (), [(keep.shape, BF16), part, part], 0, after=after)


def sort_kernel(keep_ref, *refs):
    arrived_refs, out_refs = refs[:2], refs[2:]
    for high, out_ref in enumerate(out_refs):
        for side in range(2):
            for panel in range(2):
                out_ref[panel, 2 * side] = keep_ref[side, panel, high]
                out_ref[panel, 2 * side + 1] = arrived_refs[panel][side, high]


def sort(line, keep, arrived):
    groups, share, width = keep.shape[2:]
    return call(line, sort_kernel, "sort", (keep, *arrived), (), [((2, 4, share, width), BF16)] * groups, 0)


def far_blocks(blocks):
    size = 4 * len(blocks)
    return [blocks[0]] + [swap(b, "tp", 4 * h, size) for h, b in enumerate(blocks) if h]


def expanding_kernel(*refs):
    out_ref = refs[-1]
    for high, ref in enumerate(refs[:-1]):
        for source in range(4):
            out_ref[4 * high + source] = ref[1, source]


def expanding(line, blocks):
    share, width = blocks[0].shape[2:]
    out = [((4 * len(blocks), share, width), BF16)]
    return call(line, expanding_kernel, "expanding", blocks, (), out, 0)[0]


def owners(ids, shape, high, share):
    owner = 4 * high + lax.broadcasted_iota(jnp.int32, shape, 1) // share
    return owner == (ids ^ lax.axis_index("tp"))


def shrink_kernel(steps, groups, *refs):
    panels, attended, out_refs = refs[:groups], refs[groups:-2], refs[-2:]
    share, width = panels[0].shape[2:]
    for k, a_ref in enumerate(attended):
        rows = a_ref.shape[0] - GROUP_REQ
        requests = rows // steps
        row = lax.broadcasted_iota(jnp.int32, (requests, requests), 0)
        column = lax.broadcasted_iota(jnp.int32, (requests, requests), 1)
        line = a_ref[rows : rows + GROUP_REQ, :requests].astype(F32)[:1, :]
        ids = jnp.where(row == column, line, 0.0).sum(1, keepdims=True).astype(jnp.int32)
        ids = jnp.concatenate([ids] * steps, 0)
        total = None
        for high, panel in enumerate(panels):
            flat = panel[0].reshape(4 * share, width)
            ranks = lax.dot_general(
                a_ref[:rows, :], flat, (((1,), (1,)), ((), ())), preferred_element_type=F32
            )
            ranks = jnp.where(owners(ids, ranks.shape, high, share), ranks, 0.0)
            total = ranks if total is None else total + ranks
        part = total[:, :share]
        for i in range(1, 4):
            part = part + total[:, share * i : share * (i + 1)]
        fold = out_refs[0].shape[1]
        part = jnp.concatenate([part[i * fold : (i + 1) * fold] for i in range(rows // fold)], 1)
        for out_ref in out_refs:
            out_ref[k] = part.astype(out_ref.dtype)


def shrink(line, steps, panels, attended):
    replicas, rows, share = len(attended), attended[0].shape[0] - GROUP_REQ, panels[0].shape[2]
    return call(
        line,
        functools.partial(shrink_kernel, steps, len(panels)),
        "shrink",
        (*panels, *attended),
        (),
        [((replicas, rows * share // LANES, LANES), dtype) for dtype in (F32, BF16)],
        2 * rows * replicas * len(panels) * panels[0].size,
    )


def expand_kernel(steps, replicas, ids_ref, *refs):
    ranks, panels, out_ref = refs[:replicas], refs[replicas:-1], refs[-1]
    _, share, width = panels[0].shape
    ids = jnp.concatenate([ids_ref[...]] * steps, 0)
    total = None
    for k, rank_ref in enumerate(ranks):
        folded = rank_ref[...].astype(F32)
        part = jnp.concatenate([folded[:, i * share : (i + 1) * share] for i in range(LANES // share)], 0)
        part = jnp.concatenate([part] * 4, 1)
        panel = panels[k]
        spread = [
            jnp.where(owners(ids, part.shape, high, share), part, 0.0).astype(BF16)
            for high in range(panel.shape[0] // 4)
        ]
        term = jnp.dot(
            jnp.concatenate(spread, 1), panel[...].reshape(-1, width), preferred_element_type=F32
        )
        total = term if total is None else total + term
    out_ref[...] = total


def expand(line, steps, ids, ranks, panels):
    rows, width = steps * ids.shape[0], panels[0].shape[2]
    return call(
        line,
        functools.partial(expand_kernel, steps, len(ranks)),
        "expand",
        (ids, *ranks, *panels),
        (),
        [((rows, width), F32)],
        2 * rows * len(panels) * panels[0].size,
    )[0]


def fold_kernel(keep_ref, arrived_ref, out_ref):
    out_ref[...] = keep_ref[0] + arrived_ref[0, : keep_ref.shape[1], :].astype(F32)


def fold(line, terms):
    return call(line, fold_kernel, "fold", terms, (), [(terms[0].shape[1:], F32)], 0)[0]


def finish_kernel(spans, folded, lora_ref, *refs):
    refs, out_ref = refs[:-1], refs[-1]
    for n, span in enumerate(spans):
        if n < folded:
            total = refs[n][...]
        else:
            keep_ref, arrived_ref = refs[2 * n - folded : 2 * n - folded + 2]
            total = keep_ref[0] + arrived_ref[0, : keep_ref.shape[1], :].astype(F32)
        out_ref[span, :] = (total + lora_ref[span, :]).astype(BF16)


def finish(spans, lora, sums, terms):
    operands = [pltpu.with_memory_space_constraint(x, pltpu.VMEM) for x in (lora, *sums, *terms)]
    return pl.pallas_call(
        functools.partial(finish_kernel, spans, len(sums)),
        in_specs=[pl.BlockSpec(memory_space=pltpu.VMEM)] * len(operands),
        out_specs=pl.BlockSpec(memory_space=pltpu.VMEM),
        out_shape=jax.ShapeDtypeStruct(lora.shape, BF16),
        compiler_params=pltpu.CompilerParams(vmem_limit_bytes=VMEM_LIMIT),
        cost_estimate=pl.CostEstimate(flops=4 * lora.size, bytes_accessed=1 << 20, transcendentals=0),
        name="finish",
    )(*operands)


def swap(array, axis, bit, size):
    return lax.ppermute(array, axis, [(i, i ^ bit) for i in range(size)])


def body(
    size,
    replicas,
    queries,
    key_cache,
    value_cache,
    new_keys,
    new_values,
    cache_lengths,
    adapter_ids,
    out_weight,
    shrink_panels,
    expand_panels,
):
    steps, requests, local = queries.shape
    rows = steps * requests
    pairs = size // 2
    stages = size.bit_length() - 2
    if stages == 3:
        plan, first_piece, ride, steps_list = PLAN, FIRST_PIECE, RIDE, STEPS
    else:
        plan, first_piece, ride, steps_list = ((16, tuple(range(stages))),), 1, 0, PLAIN_STEPS
    spans, first = [], 0
    for part, _ in plan:
        spans.append(slice(first, first + rows * part // 16))
        first += rows * part // 16

    line = []
    last = len(plan) - 1
    keeps, cames, sums = {}, {}, {}

    def chunk(n):
        piece = 0 if n < first_piece else 1
        start = spans[first_piece].start if piece else 0
        there = slice(spans[n].start - start, spans[n].stop - start)
        return (spans[n], there), (attended, attended_other[piece], weight_own, weight_other)

    def begin(n):
        rows, operands = chunk(n)
        order = plan[n][1]
        block = far(line, rows, order[0], operands, sent if n == ride else None)
        cames[n] = swap(block, "tp", 2 << order[0], size)

    def middle(n):
        nonlocal shrunk
        rows, operands = chunk(n)
        order = plan[n][1]
        following = order[1] - (order[1] > order[0])
        *more, keeps[n], send = near(
            line, rows, order[0], following, operands, cames[n], shrunk if n == ride else None
        )
        shrunk = more[0] if more else shrunk
        cames[n] = swap(send, "tp", 2 << order[1], size)

    def end(n):
        nonlocal shrunk
        order = plan[n][1]
        for i in range(2, len(order)):
            left = order[i] - sum(order[i] > t for t in order[:i])
            *more, keeps[n], send = add(line, left, keeps[n], cames[n], shrunk if n == ride else None)
            shrunk = more[0] if more else shrunk
            cames[n] = swap(send, "tp", 2 << order[i], size)
        sums[n] = [keeps[n], cames[n]]

    picked, cut_keep, cut_send = pick(line, out_weight, shrink_panels, expand_panels, size, replicas)
    weight_other = swap(picked, "tp", 1, size)
    cut_came = swap(cut_send, "tp", 2, size)
    pieces = [spans[first_piece - 1].stop]
    if first_piece < len(plan):
        pieces.append(rows - pieces[0])
    attended, weight_own, *attended_pieces = attend(
        line, queries, key_cache, value_cache, new_keys, new_values, cache_lengths, adapter_ids, out_weight, size, pieces
    )
    attended_other = [swap(piece, "tp", 1, size) for piece in attended_pieces]
    attended_all = [attended] + [swap(attended, "rep", k, replicas) for k in range(1, replicas)]

    shrunk = sent = panels = ranks = lora = None
    expanding_all = []
    for step in steps_list:
        name, n = (step[:-1], int(step[-1])) if step[-1].isdigit() else (step, 0)
        if name == "side":
            side_keep, *side_send = side(line, cut_keep, cut_came, ())
        elif name == "far":
            begin(n)
        elif name == "sort":
            panels = far_blocks(sort(line, side_keep, [swap(part, "tp", 1, size) for part in side_send]))
        elif name == "shrink":
            shrunk, sent = shrink(line, steps, panels, attended_all)
        elif name == "core":
            shrunk, *parts = total(line, shrunk, swap(sent, "tp", 1, size))
            parts = [swap(part, "rep", k + 1, replicas) for k, part in enumerate(parts)]
        elif name == "cross":
            shrunk, sent = cross(line, shrunk, parts)
        elif name == "ranks":
            rows_there = spans[ride].stop - spans[ride].start
            ranks = arrive(line, rows_there, shrunk, cames[ride])
        elif name == "near":
            middle(n)
        elif name == "end":
            end(n)
        elif name == "fold":
            sums[n] = [fold(line, sums[n])]
        elif name == "expanding":
            expanding_all = [expanding(line, panels)]
            expanding_all += [swap(expanding_all[0], "rep", k, replicas) for k in range(1, replicas)]
        elif name == "expand":
            lora = expand(line, steps, adapter_ids, ranks, expanding_all)
        elif name == "have_x":
            line += attended_all[1:]
        elif name == "have_e":
            line += expanding_all[1:]
        elif name == "have":
            line.append(cames[n])
    order = sorted(range(last + 1), key=lambda n: len(sums[n]))
    ready = [sums[n][0] for n in order if len(sums[n]) == 1]
    terms = [x for n in order if len(sums[n]) == 2 for x in sums[n]]
    return finish([spans[n] for n in order], lora, ready, terms).reshape(queries.shape)


def solution(mesh):
    return jax.shard_map(
        functools.partial(body, mesh.shape["tp"], mesh.shape["rep"]),
        mesh=mesh,
        in_specs=(
            P(None, "rep", "tp"),
            P("rep", None, None),
            P("rep", None, None),
            P(None, "rep", None),
            P(None, "rep", None),
            P("rep"),
            P("rep", None),
            P("tp", None),
            P("tp", None, None),
            P("tp", None, None),
        ),
        out_specs=P(None, "rep", "tp"),
        check_vma=False,
    )
```

```python
import functools

import jax
import jax.numpy as jnp
from jax import lax
from jax.experimental import pallas as pl
from jax.experimental.pallas import tpu as pltpu
from jax.sharding import PartitionSpec as P

HD = 128
LANES = 128
GROUP_REQ = 16
VMEM_LIMIT = 24 << 20
F32 = jnp.float32
BF16 = jnp.bfloat16
PLAN = ((8, (0, 1, 2)), (4, (0, 1, 2)), (1, (0, 1, 2)), (3, (1, 0, 2)))
FIRST_PIECE = 4
RIDE = 2
STEPS = (
    "side",
    "far3",
    "far0",
    "sort",
    "have_x",
    "far1",
    "have3",
    "near0",
    "shrink",
    "core",
    "cross",
    "expanding",
    "far2",
    "near1",
    "end0",
    "near3",
    "near2",
    "end2",
    "end1",
    "fold0",
    "end3",
    "ranks",
    "expand",
    "fold1",
    "fold3",
)
PLAIN_STEPS = ("side", "sort", "shrink", "core", "cross", "far0", "near0", "end0", "ranks", "expanding", "expand")


def call(line, kernel, name, vmem, hbm, out, cost, scratch=(), after=()):
    operands = [pltpu.with_memory_space_constraint(x, pltpu.VMEM) for x in vmem]
    operands += [pltpu.with_memory_space_constraint(x, pltpu.HBM) for x in hbm]
    before = [*line, *after]
    count, extra = len(operands), len(before)

    def run(*refs):
        kernel(*refs[:count], *refs[count + extra :])

    results = pl.pallas_call(
        run,
        in_specs=[pl.BlockSpec(memory_space=pltpu.VMEM)] * len(vmem)
        + [pl.BlockSpec(memory_space=pltpu.HBM)] * len(hbm)
        + [pl.BlockSpec(memory_space=pl.ANY)] * extra,
        out_specs=[pl.BlockSpec(memory_space=pltpu.VMEM)] * len(out),
        out_shape=[pltpu.VMEM(shape, dtype) for shape, dtype in out],
        scratch_shapes=scratch,
        compiler_params=pltpu.CompilerParams(vmem_limit_bytes=VMEM_LIMIT),
        cost_estimate=pl.CostEstimate(flops=cost, bytes_accessed=1 << 16, transcendentals=0),
        name=name,
    )(*operands, *before)
    line[:] = [min(results, key=lambda x: x.size)]
    return results


def put_bit(i, position, value):
    low = i & ((1 << position) - 1)
    return ((i >> position) << (position + 1)) | (value << position) | low


def cut_copies(panel_ref, keep_ref, send_ref, panel, place, replica):
    groups, share, width = keep_ref.shape[2:]
    rank = pl.multiple_of(replica * share, share)
    copies = []
    for low, cut_ref in enumerate((keep_ref, keep_ref, send_ref, send_ref)):
        for high in range(groups):
            column = pl.multiple_of((place ^ (4 * high + low)) * width, width)
            copies.append(
                (panel_ref.at[0, pl.ds(rank, share), pl.ds(column, width)], cut_ref.at[low % 2, panel, high])
            )
    return copies


def run_copies(copies, sems):
    copies = [pltpu.make_async_copy(a, b, sems.at[i]) for i, (a, b) in enumerate(copies)]
    for copy in copies:
        copy.start()
    for copy in copies:
        copy.wait()


def pick_kernel(w_ref, shrink_ref, expand_ref, pick_ref, keep_ref, send_ref, sems):
    place, replica = lax.axis_index("tp"), lax.axis_index("rep")
    pairs, _, width = pick_ref.shape
    copies = []
    for i in range(pairs):
        column = pl.multiple_of((2 * (i ^ (place // 2)) + 1 - place % 2) * width, width)
        copies.append((w_ref.at[:, pl.ds(column, width)], pick_ref.at[i]))
    copies += cut_copies(shrink_ref, keep_ref, send_ref, 0, place, replica)
    copies += cut_copies(expand_ref, keep_ref, send_ref, 1, place, replica)
    run_copies(copies, sems)


def pick(line, weight, shrink_panels, expand_panels, size, replicas):
    depth, full = weight.shape
    pairs, width = size // 2, full // size
    cut = ((2, 2, size // 4, shrink_panels.shape[1] // replicas, width), BF16)
    return call(
        line,
        pick_kernel,
        "pick",
        (),
        (weight, shrink_panels, expand_panels),
        [((pairs, depth, width), BF16), cut, cut],
        0,
        scratch=[pltpu.SemaphoreType.DMA((pairs + 2 * size,))],
    )


def attention_kernel(
    lengths_ref, ids_ref, q_hbm, kc_hbm, vc_hbm, nk_hbm, nv_hbm, w_hbm, out_ref, own_ref, *rest
):
    *piece_refs, q_ref, kc_ref, vc_ref, nk_ref, nv_ref, q_sems, w_sems = rest
    place = lax.axis_index("tp")
    steps, requests, width = q_ref.shape
    heads = width // HD
    cached, fresh = kc_ref.shape[0], nk_ref.shape[0]
    block = own_ref.shape[2]
    size = 2 * own_ref.shape[0]
    group_heads = size * width // kc_hbm.shape[2]
    head = pl.multiple_of(place * heads // group_heads * HD, HD)
    parts = 2
    part = requests // parts
    loads = []
    for n in range(parts):
        span = pl.ds(n * part, part)
        pieces = [(q_hbm.at[:, span, :], q_ref.at[:, span, :])]
        for a, b in ((kc_hbm, kc_ref), (nk_hbm, nk_ref), (vc_hbm, vc_ref), (nv_hbm, nv_ref)):
            pieces.append((a.at[:, span, pl.ds(head, HD)], b.at[:, span, :]))
        loads.append([pltpu.make_async_copy(a, b, q_sems.at[n, i]) for i, (a, b) in enumerate(pieces)])
    pair, mine = place // 2, place % 2
    others = []
    for i in range(own_ref.shape[0]):
        column = pl.multiple_of((2 * (i ^ pair) + mine) * block, block)
        others.append((w_hbm.at[:, pl.ds(column, block)], own_ref.at[i]))
    others = [pltpu.make_async_copy(a, b, w_sems.at[i]) for i, (a, b) in enumerate(others)]
    for copy in [c for load in loads for c in load] + others:
        copy.start()

    group = GROUP_REQ
    rows, columns = steps * heads * group, (cached + fresh) * group
    row = lax.broadcasted_iota(jnp.int32, (rows, columns), 0)
    column = lax.broadcasted_iota(jnp.int32, (rows, columns), 1)
    same = row % group == column % group
    position = column // group
    step = row // (heads * group)
    fresh_ok = jnp.logical_and(position >= cached, position - cached <= step)
    column_position = lax.broadcasted_iota(jnp.int32, (1, columns), 1) // group
    tail = lax.broadcasted_iota(jnp.int32, (group, requests), 0) == 0
    out_ref[steps * requests :, :] = jnp.zeros((group, width), BF16)
    out_ref[steps * requests :, :requests] = jnp.where(tail, ids_ref[...].astype(F32), 0.0).astype(BF16)
    for n in range(parts):
        for copy in loads[n]:
            copy.wait()
        for i in range(n * part // group, (n + 1) * part // group):
            span = slice(i * group, (i + 1) * group)
            query = jnp.concatenate(
                [q_ref[s, span, h * HD : (h + 1) * HD] for s in range(steps) for h in range(heads)], 0
            )
            keys = jnp.concatenate(
                [kc_ref[p, span, :] for p in range(cached)] + [nk_ref[s, span, :] for s in range(fresh)], 0
            )
            values = jnp.concatenate(
                [vc_ref[p, span, :] for p in range(cached)] + [nv_ref[s, span, :] for s in range(fresh)], 0
            )
            scores = lax.dot_general(
                query, keys, (((1,), (1,)), ((), ())), preferred_element_type=F32
            ) * (1.0 / HD**0.5)
            limit = jnp.concatenate([lengths_ref[:, span]] * (cached + fresh), 1)
            cached_ok = column_position < limit
            visible = jnp.logical_and(same, jnp.logical_or(cached_ok, fresh_ok))
            scores = jnp.where(visible, scores, -1e30)
            scaled = jnp.exp(scores - scores.max(-1, keepdims=True))
            weights = (scaled / scaled.sum(-1, keepdims=True)).astype(BF16)
            mixed = jnp.dot(weights, values, preferred_element_type=F32).astype(BF16)
            for s in range(steps):
                for h in range(heads):
                    at = (s * heads + h) * group
                    to = s * requests + i * group
                    out_ref[to : to + group, h * HD : (h + 1) * HD] = mixed[at : at + group, :]
    first = 0
    for piece_ref in piece_refs:
        piece_ref[...] = out_ref[first : first + piece_ref.shape[0], :]
        first += piece_ref.shape[0]
    for copy in others:
        copy.wait()


def attend(line, queries, key_cache, value_cache, new_keys, new_values, cache_lengths, adapter_ids, weight, size, pieces):
    steps, requests, width = queries.shape
    cached = key_cache.shape[1]
    depth, full = weight.shape
    block, pairs = full // size, size // 2
    return call(
        line,
        attention_kernel,
        "attention",
        (cache_lengths.reshape(1, -1), adapter_ids.reshape(1, -1)),
        (queries, key_cache.transpose(1, 0, 2), value_cache.transpose(1, 0, 2), new_keys, new_values, weight),
        [
            ((steps * requests + GROUP_REQ, width), BF16),
            ((pairs, depth, block), BF16),
        ]
        + [((piece, width), BF16) for piece in pieces],
        4 * requests * steps * width * (cached + steps) * GROUP_REQ,
        [
            pltpu.VMEM((steps, requests, width), BF16),
            pltpu.VMEM((cached, requests, HD), BF16),
            pltpu.VMEM((cached, requests, HD), BF16),
            pltpu.VMEM((steps, requests, HD), BF16),
            pltpu.VMEM((steps, requests, HD), BF16),
            pltpu.SemaphoreType.DMA((2, 5)),
            pltpu.SemaphoreType.DMA((pairs,)),
        ],
    )


def product(spans, which, a_ref, b_ref, own_ref, other_ref):
    return jnp.dot(a_ref[spans[0], :], own_ref[which], preferred_element_type=F32) + jnp.dot(
        b_ref[spans[1], :], other_ref[which], preferred_element_type=F32
    )


def pack(small, blocks, width):
    part = small.shape[0] // blocks
    fold = part * LANES // width
    return [
        jnp.concatenate([small[i * part + j : i * part + j + fold] for j in range(0, part, fold)], 1)
        for i in range(blocks)
    ]


def unpack(blocks):
    return jnp.concatenate(
        [block[:, j : j + LANES] for block in blocks for j in range(0, block.shape[1], LANES)], 0
    )


def extra_rows(small, blocks, width):
    return 0 if small is None else small.size // (blocks * width)


def pass_small(small_ref, arrived_ref, more_ref, send_ref, rows):
    flat = small_ref[...].reshape(-1, LANES)
    flat = flat + unpack([arrived_ref[i, rows:, :].astype(F32) for i in range(arrived_ref.shape[0])])
    more_ref[...] = flat.reshape(more_ref.shape)
    if send_ref is not None:
        for i, block in enumerate(pack(flat.astype(BF16), send_ref.shape[0], send_ref.shape[2])):
            send_ref[i, rows:, :] = block


def far_kernel(spans, stage, *refs):
    operands, sent_refs, out_ref = refs[:4], refs[4:-1], refs[-1]
    rows = spans[0].stop - spans[0].start
    for i in range(out_ref.shape[0]):
        out_ref[i, :rows, :] = product(spans, put_bit(i, stage, 1), *operands).astype(BF16)
    for sent_ref in sent_refs:
        for i, block in enumerate(pack(sent_ref[...].reshape(-1, LANES), out_ref.shape[0], out_ref.shape[2])):
            out_ref[i, rows:, :] = block


def far(line, spans, stage, operands, sent=None):
    pairs, depth, width = operands[2].shape
    rows = spans[0].stop - spans[0].start
    more = extra_rows(sent, pairs // 2, width)
    return call(
        line,
        functools.partial(far_kernel, spans, stage),
        "far",
        operands if sent is None else (*operands, sent),
        (),
        [((pairs // 2, rows + more, width), BF16)],
        2 * rows * depth * pairs * width,
    )[0]


def near_kernel(spans, stage, following, *refs):
    operands, arrived_ref, refs = refs[:4], refs[4], refs[5:]
    rows = spans[0].stop - spans[0].start
    keep_ref, send_ref = refs[-2:]
    for i in range(keep_ref.shape[0]):
        for value, out_ref in ((1, send_ref), (0, keep_ref)):
            at = put_bit(i, following, value)
            total = product(spans, put_bit(at, stage, 0), *operands) + arrived_ref[at, :rows, :].astype(F32)
            out_ref[i, :rows, :] = total.astype(out_ref.dtype)
    if len(refs) > 2:
        pass_small(refs[0], arrived_ref, refs[1], send_ref, rows)


def near(line, spans, stage, following, operands, arrived, small=None):
    pairs, depth, width = operands[2].shape
    rows = spans[0].stop - spans[0].start
    more = extra_rows(small, pairs // 4, width)
    return call(
        line,
        functools.partial(near_kernel, spans, stage, following),
        "near",
        (*operands, arrived) if small is None else (*operands, arrived, small),
        (),
        ([] if small is None else [(small.shape, F32)])
        + [((pairs // 4, rows, width), F32), ((pairs // 4, rows + more, width), BF16)],
        2 * rows * depth * pairs * width,
    )


def add_kernel(following, keep_ref, arrived_ref, *refs):
    more_ref, send_ref = refs[-2:]
    rows = keep_ref.shape[1]
    for i in range(more_ref.shape[0]):
        for value, out_ref in ((1, send_ref), (0, more_ref)):
            at = put_bit(i, following, value)
            total = keep_ref[at] + arrived_ref[at, :rows, :].astype(F32)
            out_ref[i, :rows, :] = total.astype(out_ref.dtype)
    if len(refs) > 2:
        pass_small(refs[0], arrived_ref, refs[1], send_ref, rows)


def add(line, following, keep, arrived, small=None):
    blocks, rows, width = keep.shape
    more = extra_rows(small, blocks // 2, width)
    return call(
        line,
        functools.partial(add_kernel, following),
        "add",
        (keep, arrived) if small is None else (keep, arrived, small),
        (),
        ([] if small is None else [(small.shape, F32)])
        + [((blocks // 2, rows, width), F32), ((blocks // 2, rows + more, width), BF16)],
        2 * keep.size,
    )


def total_kernel(a_ref, b_ref, out_ref, *sent_refs):
    out_ref[...] = a_ref[...] + b_ref[...].astype(F32)
    for k, sent_ref in enumerate(sent_refs):
        sent_ref[...] = out_ref[k + 1].astype(BF16)


def total(line, a, b):
    out = [(a.shape, F32)] + [(a.shape[1:], BF16)] * (a.shape[0] - 1)
    return call(line, total_kernel, "total", (a, b), (), out, a.size)


def cross_kernel(a_ref, *refs):
    arrived_refs, (out_ref, sent_ref) = refs[:-2], refs[-2:]
    out_ref[0] = a_ref[0]
    for k, ref in enumerate(arrived_refs):
        out_ref[k + 1] = ref[...].astype(F32)
    sent_ref[...] = out_ref[...].astype(BF16)


def cross(line, a, arrived):
    return call(line, cross_kernel, "cross", (a, *arrived), (), [(a.shape, F32), (a.shape, BF16)], 0)


def arrive_kernel(rows, small_ref, arrived_ref, *out_refs):
    flat = small_ref[...].reshape(-1, LANES) + unpack([arrived_ref[0, rows:, :].astype(F32)])
    small = flat.reshape(small_ref.shape).astype(BF16)
    for k, out_ref in enumerate(out_refs):
        out_ref[...] = small[k]


def arrive(line, rows, small, arrived):
    out = [(small.shape[1:], BF16)] * small.shape[0]
    return call(line, functools.partial(arrive_kernel, rows), "arrive", (small, arrived), (), out, 0)


def side_kernel(keep_ref, arrived_ref, more_ref, *send_refs):
    for source, ref in enumerate((keep_ref, arrived_ref)):
        more_ref[source] = ref[0]
        for panel, send_ref in enumerate(send_refs):
            send_ref[source] = ref[1, panel]


def side(line, keep, arrived, after):
    part = (keep.shape[:1] + keep.shape[2:], BF16)
    return call(line, side_kernel, "side", (keep, arrived), (), [(keep.shape, BF16), part, part], 0, after=after)


def sort_kernel(keep_ref, *refs):
    arrived_refs, out_refs = refs[:2], refs[2:]
    for high, out_ref in enumerate(out_refs):
        for side in range(2):
            for panel in range(2):
                out_ref[panel, 2 * side] = keep_ref[side, panel, high]
                out_ref[panel, 2 * side + 1] = arrived_refs[panel][side, high]


def sort(line, keep, arrived):
    groups, share, width = keep.shape[2:]
    return call(line, sort_kernel, "sort", (keep, *arrived), (), [((2, 4, share, width), BF16)] * groups, 0)


def far_blocks(blocks):
    size = 4 * len(blocks)
    return [blocks[0]] + [swap(b, "tp", 4 * h, size) for h, b in enumerate(blocks) if h]


def expanding_kernel(*refs):
    out_ref = refs[-1]
    for high, ref in enumerate(refs[:-1]):
        for source in range(4):
            out_ref[4 * high + source] = ref[1, source]


def expanding(line, blocks):
    share, width = blocks[0].shape[2:]
    out = [((4 * len(blocks), share, width), BF16)]
    return call(line, expanding_kernel, "expanding", blocks, (), out, 0)[0]


def owners(ids, shape, high, share):
    owner = 4 * high + lax.broadcasted_iota(jnp.int32, shape, 1) // share
    return owner == (ids ^ lax.axis_index("tp"))


def shrink_kernel(steps, groups, *refs):
    panels, attended, out_refs = refs[:groups], refs[groups:-2], refs[-2:]
    share, width = panels[0].shape[2:]
    for k, a_ref in enumerate(attended):
        rows = a_ref.shape[0] - GROUP_REQ
        requests = rows // steps
        row = lax.broadcasted_iota(jnp.int32, (requests, requests), 0)
        column = lax.broadcasted_iota(jnp.int32, (requests, requests), 1)
        line = a_ref[rows : rows + GROUP_REQ, :requests].astype(F32)[:1, :]
        ids = jnp.where(row == column, line, 0.0).sum(1, keepdims=True).astype(jnp.int32)
        ids = jnp.concatenate([ids] * steps, 0)
        total = None
        for high, panel in enumerate(panels):
            flat = panel[0].reshape(4 * share, width)
            ranks = lax.dot_general(
                a_ref[:rows, :], flat, (((1,), (1,)), ((), ())), preferred_element_type=F32
            )
            ranks = jnp.where(owners(ids, ranks.shape, high, share), ranks, 0.0)
            total = ranks if total is None else total + ranks
        part = total[:, :share]
        for i in range(1, 4):
            part = part + total[:, share * i : share * (i + 1)]
        fold = out_refs[0].shape[1]
        part = jnp.concatenate([part[i * fold : (i + 1) * fold] for i in range(rows // fold)], 1)
        for out_ref in out_refs:
            out_ref[k] = part.astype(out_ref.dtype)


def shrink(line, steps, panels, attended):
    replicas, rows, share = len(attended), attended[0].shape[0] - GROUP_REQ, panels[0].shape[2]
    return call(
        line,
        functools.partial(shrink_kernel, steps, len(panels)),
        "shrink",
        (*panels, *attended),
        (),
        [((replicas, rows * share // LANES, LANES), dtype) for dtype in (F32, BF16)],
        2 * rows * replicas * len(panels) * panels[0].size,
    )


def expand_kernel(steps, replicas, ids_ref, *refs):
    ranks, panels, out_ref = refs[:replicas], refs[replicas:-1], refs[-1]
    _, share, width = panels[0].shape
    ids = jnp.concatenate([ids_ref[...]] * steps, 0)
    total = None
    for k, rank_ref in enumerate(ranks):
        folded = rank_ref[...].astype(F32)
        part = jnp.concatenate([folded[:, i * share : (i + 1) * share] for i in range(LANES // share)], 0)
        part = jnp.concatenate([part] * 4, 1)
        panel = panels[k]
        spread = [
            jnp.where(owners(ids, part.shape, high, share), part, 0.0).astype(BF16)
            for high in range(panel.shape[0] // 4)
        ]
        term = jnp.dot(
            jnp.concatenate(spread, 1), panel[...].reshape(-1, width), preferred_element_type=F32
        )
        total = term if total is None else total + term
    out_ref[...] = total


def expand(line, steps, ids, ranks, panels):
    rows, width = steps * ids.shape[0], panels[0].shape[2]
    return call(
        line,
        functools.partial(expand_kernel, steps, len(ranks)),
        "expand",
        (ids, *ranks, *panels),
        (),
        [((rows, width), F32)],
        2 * rows * len(panels) * panels[0].size,
    )[0]


def fold_kernel(keep_ref, arrived_ref, out_ref):
    out_ref[...] = keep_ref[0] + arrived_ref[0, : keep_ref.shape[1], :].astype(F32)


def fold(line, terms):
    return call(line, fold_kernel, "fold", terms, (), [(terms[0].shape[1:], F32)], 0)[0]


def finish_kernel(spans, folded, lora_ref, *refs):
    refs, out_ref = refs[:-1], refs[-1]
    for n, span in enumerate(spans):
        if n < folded:
            total = refs[n][...]
        else:
            keep_ref, arrived_ref = refs[2 * n - folded : 2 * n - folded + 2]
            total = keep_ref[0] + arrived_ref[0, : keep_ref.shape[1], :].astype(F32)
        out_ref[span, :] = (total + lora_ref[span, :]).astype(BF16)


def finish(spans, lora, sums, terms):
    operands = [pltpu.with_memory_space_constraint(x, pltpu.VMEM) for x in (lora, *sums, *terms)]
    return pl.pallas_call(
        functools.partial(finish_kernel, spans, len(sums)),
        in_specs=[pl.BlockSpec(memory_space=pltpu.VMEM)] * len(operands),
        out_specs=pl.BlockSpec(memory_space=pltpu.VMEM),
        out_shape=jax.ShapeDtypeStruct(lora.shape, BF16),
        compiler_params=pltpu.CompilerParams(vmem_limit_bytes=VMEM_LIMIT),
        cost_estimate=pl.CostEstimate(flops=4 * lora.size, bytes_accessed=1 << 20, transcendentals=0),
        name="finish",
    )(*operands)


def swap(array, axis, bit, size):
    return lax.ppermute(array, axis, [(i, i ^ bit) for i in range(size)])


def body(
    size,
    replicas,
    queries,
    key_cache,
    value_cache,
    new_keys,
    new_values,
    cache_lengths,
    adapter_ids,
    out_weight,
    shrink_panels,
    expand_panels,
):
    steps, requests, local = queries.shape
    rows = steps * requests
    pairs = size // 2
    stages = size.bit_length() - 2
    if stages == 3:
        plan, first_piece, ride, steps_list = PLAN, FIRST_PIECE, RIDE, STEPS
    else:
        plan, first_piece, ride, steps_list = ((16, tuple(range(stages))),), 1, 0, PLAIN_STEPS
    spans, first = [], 0
    for part, _ in plan:
        spans.append(slice(first, first + rows * part // 16))
        first += rows * part // 16

    line = []
    last = len(plan) - 1
    keeps, cames, sums = {}, {}, {}

    def chunk(n):
        piece = 0 if n < first_piece else 1
        start = spans[first_piece].start if piece else 0
        there = slice(spans[n].start - start, spans[n].stop - start)
        return (spans[n], there), (attended, attended_other[piece], weight_own, weight_other)

    def begin(n):
        rows, operands = chunk(n)
        order = plan[n][1]
        block = far(line, rows, order[0], operands, sent if n == ride else None)
        cames[n] = swap(block, "tp", 2 << order[0], size)

    def middle(n):
        nonlocal shrunk
        rows, operands = chunk(n)
        order = plan[n][1]
        following = order[1] - (order[1] > order[0])
        *more, keeps[n], send = near(
            line, rows, order[0], following, operands, cames[n], shrunk if n == ride else None
        )
        shrunk = more[0] if more else shrunk
        cames[n] = swap(send, "tp", 2 << order[1], size)

    def end(n):
        nonlocal shrunk
        order = plan[n][1]
        for i in range(2, len(order)):
            left = order[i] - sum(order[i] > t for t in order[:i])
            *more, keeps[n], send = add(line, left, keeps[n], cames[n], shrunk if n == ride else None)
            shrunk = more[0] if more else shrunk
            cames[n] = swap(send, "tp", 2 << order[i], size)
        sums[n] = [keeps[n], cames[n]]

    picked, cut_keep, cut_send = pick(line, out_weight, shrink_panels, expand_panels, size, replicas)
    weight_other = swap(picked, "tp", 1, size)
    cut_came = swap(cut_send, "tp", 2, size)
    pieces = [spans[first_piece - 1].stop]
    if first_piece < len(plan):
        pieces.append(rows - pieces[0])
    attended, weight_own, *attended_pieces = attend(
        line, queries, key_cache, value_cache, new_keys, new_values, cache_lengths, adapter_ids, out_weight, size, pieces
    )
    attended_other = [swap(piece, "tp", 1, size) for piece in attended_pieces]
    attended_all = [attended] + [swap(attended, "rep", k, replicas) for k in range(1, replicas)]

    shrunk = sent = panels = ranks = lora = None
    expanding_all = []
    for step in steps_list:
        name, n = (step[:-1], int(step[-1])) if step[-1].isdigit() else (step, 0)
        if name == "side":
            side_keep, *side_send = side(line, cut_keep, cut_came, ())
        elif name == "far":
            begin(n)
        elif name == "sort":
            panels = far_blocks(sort(line, side_keep, [swap(part, "tp", 1, size) for part in side_send]))
        elif name == "shrink":
            shrunk, sent = shrink(line, steps, panels, attended_all)
        elif name == "core":
            shrunk, *parts = total(line, shrunk, swap(sent, "tp", 1, size))
            parts = [swap(part, "rep", k + 1, replicas) for k, part in enumerate(parts)]
        elif name == "cross":
            shrunk, sent = cross(line, shrunk, parts)
        elif name == "ranks":
            rows_there = spans[ride].stop - spans[ride].start
            ranks = arrive(line, rows_there, shrunk, cames[ride])
        elif name == "near":
            middle(n)
        elif name == "end":
            end(n)
        elif name == "fold":
            sums[n] = [fold(line, sums[n])]
        elif name == "expanding":
            expanding_all = [expanding(line, panels)]
            expanding_all += [swap(expanding_all[0], "rep", k, replicas) for k in range(1, replicas)]
        elif name == "expand":
            lora = expand(line, steps, adapter_ids, ranks, expanding_all)
        elif name == "have_x":
            line += attended_all[1:]
        elif name == "have_e":
            line += expanding_all[1:]
        elif name == "have":
            line.append(cames[n])
    order = sorted(range(last + 1), key=lambda n: len(sums[n]))
    ready = [sums[n][0] for n in order if len(sums[n]) == 1]
    terms = [x for n in order if len(sums[n]) == 2 for x in sums[n]]
    return finish([spans[n] for n in order], lora, ready, terms).reshape(queries.shape)


def solution(mesh):
    return jax.shard_map(
        functools.partial(body, mesh.shape["tp"], mesh.shape["rep"]),
        mesh=mesh,
        in_specs=(
            P(None, "rep", "tp"),
            P("rep", None, None),
            P("rep", None, None),
            P(None, "rep", None),
            P(None, "rep", None),
            P("rep"),
            P("rep", None),
            P("tp", None),
            P("tp", None, None),
            P("tp", None, None),
        ),
        out_specs=P(None, "rep", "tp"),
        check_vma=False,
    )
```
